1024 devices in a mesh: gx: 16 (over y, core), gy: 64 (over x, z).
Axes of the slice: x: 4, y: 8, z: 16, core: 2. Of those that a mesh axis runs over, the one named last changes fastest.
Arguments:
- couplings: bfloat16 [64, 512, 64, 320], P('gx', 'gy'), may hold values from -0.3125 to 0.3125
- prolong: bfloat16 [64, 512, 32, 128], P('gx', 'gy'), may hold values from -1.5 to 1.5
- present: int32 [64, 512, 4], P('gx', 'gy'), may hold values 0 or 1
- entries: int32 [64, 512, 5], P('gx', 'gy'), may hold values from 0 to 31
- owners: int32 [16, 2048, 1], P('gx', 'gy'), may hold values from 0 to 63; in each aligned block of 32 rows (0 to 31, 32 to 63, ..., all dimensions but the last counted through in order) at most 2 rows name the same one
- targets: int32 [16, 2048], P('gx', 'gy'), may hold values from 0 to 15
Outputs:
- coarse: bfloat16 [16, 1024, 32, 128], P('gx', 'gy')
The draws below stay inside these ranges and needn't reach their ends.
Inputs may be any that keep to these rules, and one draw needn't show every extreme that they name: `owners`: among the 32 partial blocks of one tile at most 2 have the same owner column, and some owner column is named exactly 2 times in some tile.
All inputs are finite; a program needn't handle non-finite values. No bound on the sum of `present` on one device may be relied on, other than what follows from the above.
Results may differ from the reference program's by a relative error of at most 0.014.
Values may be sent and summed in bfloat16 or wider, within the bound.
No kernel may reach another device: no remote copies, remote signals or barrier semaphores. Data moves between devices by JAX's collectives and lax.ppermute only.
A program may use at most 32 MiB of HBM per device.

```python
import math
import jax
import jax.numpy as jnp
import numpy as np
from jax import lax

B = 64
CX = 4
CY = 8
E = 32
OWN = 16
CAP = 2
NX = 64
NY = 512
N_GX = 16
N_GY = 64


def touch_ends(array, own_key, smallest, top_value):
    index_at = [jax.random.randint(jax.random.fold_in(own_key, axis), (), 0, length) for axis, length in enumerate(array.shape)]
    widest = array.shape.index(max(array.shape))
    beside = index_at[:widest] + [(index_at[widest] + 1) % array.shape[widest]] + index_at[widest + 1:]
    return array.at[tuple(index_at)].set(smallest).at[tuple(beside)].set(top_value)


def levels(stream_key, shape, cuts, least, largest):
    level, own = 1.0, jax.random.fold_in(stream_key, 6)
    for position, parts in cuts:
        heights = jnp.exp(jax.random.uniform(jax.random.fold_in(own, position), (parts,), jnp.float32, least / len(cuts), largest / len(cuts)))
        level = level * jnp.repeat(heights, shape[position] // parts).reshape([-1 if axis == position else 1 for axis in range(len(shape))])
    return level


def deal_out(stream_key, own, number, rows, amount, top, bound, skew):
    sequence = jax.random.permutation(stream_key, amount)
    crowded, ordinary = shares(amount, rows * top, bound, skew, True), shares(amount, rows * top, bound, skew, False)
    places = jnp.arange(amount)

    def named(sizes, turn):
        used = int((sizes > 0).sum())
        fixed = max(1, used // 4)
        shifted = fixed + (places - fixed + turn * (used - fixed)) % max(1, amount - fixed)
        return jnp.zeros((amount,), jnp.int32).at[sequence[jnp.where(places < fixed, places, shifted)]].set(jnp.asarray(sizes, jnp.int32))

    sizes = jnp.where(number % 4 == 0, named(crowded, number // 4), named(ordinary, number - number // 4 - 1))
    mixed = jax.random.permutation(jax.random.fold_in(own, 3), amount)
    giver, taker = mixed[0:amount // 2 * 2:2], mixed[1:amount // 2 * 2:2]
    slack = jnp.minimum(sizes[giver] - 1, bound - sizes[taker]) // 2
    slack = jnp.where((giver == sequence[0]) | (taker == sequence[0]) | (sizes[taker] == 0), 0, jnp.maximum(slack, 0))
    shifted = jax.random.randint(jax.random.fold_in(own, 4), (amount // 2,), 0, 1 << 20) % (slack + 1)
    sizes = sizes.at[giver].add(-shifted).at[taker].add(shifted)
    members = jnp.searchsorted(jnp.cumsum(sizes), jnp.arange(rows * top), side="right").astype(jnp.int32)
    grid = members.reshape(top, rows).T
    grid = grid[jax.random.permutation(jax.random.fold_in(own, 1), rows)]
    turn = jax.random.randint(jax.random.fold_in(own, 2), (rows, 1), 0, top)
    return jnp.take_along_axis(grid, (jnp.arange(top)[None, :] + turn) % top, axis=1)


def shares(number_of, total, bound, lean, full):
    weights = [(1 << 20) // math.isqrt(standing ** lean) + 1 for standing in range(1, number_of + 1)]
    largest = bound if full else min(bound, max(-(-total // number_of), total * weights[0] // sum(weights)))
    least = 1 if total - largest >= number_of - 1 else 0
    counts, spare = [largest] + [least] * (number_of - 1), total - largest - least * (number_of - 1)
    while spare > 0:
        free = [i for i in range(1, number_of) if counts[i] < largest] or [i for i in range(1, number_of) if counts[i] < bound]
        pool, budget = sum([weights[i] for i in free]), spare
        for i in free:
            addition = min(bound - counts[i], max(1, budget * weights[i] // pool), spare)
            counts[i] = counts[i] + addition
            spare = spare - addition
    return np.array(counts)


def noise(own_key, dims, scale, bound, shards=(), kind=jnp.bfloat16):
    values = scale * jax.random.normal(own_key, dims, jnp.float32)
    if shards:
        values = values * levels(own_key, dims, shards, -0.22, 0.18)
    return jnp.clip(values, -bound, bound).astype(kind)


def setup_inputs(seed: int = 0) -> dict:
    arg_keys = jax.random.split(jax.random.key(seed), 7)
    couplings = noise(arg_keys[0], (NX, NY, B, 5 * B), (5 * B) ** -0.5, 0.3125, ((0, 16), (1, 64)))
    prolong = noise(arg_keys[1], (NX, NY, B // 2, 2 * B), 0.25, 1.5, ((0, 16), (1, 64)))
    present = touch_ends((jax.random.randint(arg_keys[2], (NX, NY, 4), 0, 4) < 3).astype(jnp.int32), jax.random.fold_in(arg_keys[2], 1), 0, 1)
    entries = touch_ends(jax.random.randint(arg_keys[3], (NX, NY, 5), 0, E), jax.random.fold_in(arg_keys[3], 1), 0, E - 1).astype(jnp.int32)
    owners_keys = jax.random.split(jax.random.fold_in(arg_keys[4], 1), N_GX * (N_GY * E) // E)
    owners_turns = jax.random.permutation(jax.random.fold_in(arg_keys[4], 3), N_GX * (N_GY * E) // E)
    owners = jax.vmap(lambda own, number: deal_out(jax.random.fold_in(arg_keys[4], 2), own, number, E, N_GY, 1, CAP, 2))(owners_keys, owners_turns).reshape((N_GX, N_GY * E, 1))
    targets = touch_ends(jax.random.randint(arg_keys[5], (N_GX, N_GY * E), 0, OWN), jax.random.fold_in(arg_keys[5], 1), 0, OWN - 1).astype(jnp.int32)
    return dict(couplings=couplings, prolong=prolong, present=present, entries=entries, owners=owners, targets=targets)


def reference(couplings, prolong, present, entries, owners, targets):
    blocks_all = prolong.reshape(NX, NY, B, B)
    padded = jnp.pad(blocks_all, ((1, 1), (1, 1), (0, 0), (0, 0)))
    zero_index = jnp.zeros((), jnp.int32)

    def tile_terms(tile_index):
        tile_x = (tile_index // N_GY).astype(jnp.int32)
        tile_y = (tile_index % N_GY).astype(jnp.int32)
        start_x = (tile_x * CX).astype(jnp.int32)
        start_y = (tile_y * CY).astype(jnp.int32)
        window = lax.dynamic_slice(padded, (start_x, start_y, zero_index, zero_index), (CX + 2, CY + 2, B, B))
        operator = lax.dynamic_slice(couplings, (start_x, start_y, zero_index, zero_index), (CX, CY, B, 5 * B))
        operator = operator.reshape(CX, CY, B, 5, B)
        mask_tile = lax.dynamic_slice(present, (start_x, start_y, zero_index), (CX, CY, 4))
        entry_tile = lax.dynamic_slice(entries, (start_x, start_y, zero_index), (CX, CY, 5))
        own_block = window[1:-1, 1:-1]
        neighbours = jnp.stack([own_block, window[2:, 1:-1], window[:-2, 1:-1], window[1:-1, 2:], window[1:-1, :-2]], axis=2)
        factor = jnp.concatenate([jnp.ones((CX, CY, 1), jnp.float32), mask_tile.astype(jnp.float32)], axis=2)
        images = jnp.einsum('xyrdk,xydkc->xydrc', operator.astype(jnp.float32), neighbours.astype(jnp.float32))
        images = (images * factor[:, :, :, None, None]).astype(jnp.bfloat16)
        terms = jnp.einsum('xykr,xydkc->xydrc', own_block.astype(jnp.float32), images.astype(jnp.float32))
        flat_terms = terms.reshape(CX * CY * 5, B * B)
        return jax.ops.segment_sum(flat_terms, entry_tile.reshape(CX * CY * 5), num_segments=E).astype(jnp.bfloat16)

    partials = lax.map(tile_terms, jnp.arange(N_GX * N_GY, dtype=jnp.int32))
    partials = partials.reshape(N_GX, N_GY * E, B * B)
    segment_ids = (owners[:, :, 0] * OWN + targets).astype(jnp.int32)

    def row_sum(row_index):
        row_parts = partials[row_index].astype(jnp.float32)
        return jax.ops.segment_sum(row_parts, segment_ids[row_index], num_segments=N_GY * OWN).astype(jnp.bfloat16)

    coarse = lax.map(row_sum, jnp.arange(N_GX, dtype=jnp.int32))
    return coarse.reshape(N_GX, N_GY * OWN, B // 2, 2 * B)
```

```python
import jax
import jax.numpy as jnp
from jax import lax
from jax.experimental import pallas as pl
from jax.experimental.pallas import tpu as pltpu
from jax.sharding import PartitionSpec as P

RING = 16
SLOTS = 8
VMEM = pl.BlockSpec(memory_space=pltpu.VMEM)
SMEM = pl.BlockSpec(memory_space=pltpu.SMEM)
PARAMS = pltpu.CompilerParams(vmem_limit_bytes=40 * 1024 * 1024)


def unpacked(lines, wide_ref):
    lines = lines.astype(jnp.float32)
    wide_ref[pl.ds(0, 32, stride=2), :] = lines
    wide_ref[pl.ds(1, 32, stride=2), :] = pltpu.roll(lines, 64, 1)
    return wide_ref[...].astype(jnp.bfloat16)


def left_kernel(prolong_ref, couplings_ref, left_ref, rows_ref, wide_ref):
    for cell in range(prolong_ref.shape[0]):
        rows = unpacked(prolong_ref[cell], wide_ref.at[cell % 4])
        rows_ref[cell] = rows
        product = lax.dot_general(
            rows[:, :64],
            couplings_ref[cell],
            (((0,), (0,)), ((), ())),
            preferred_element_type=jnp.float32,
        ).astype(jnp.bfloat16)
        for d in range(5):
            left_ref[cell, d] = product[:, d * 64 : d * 64 + 64]


def partial_kernel(
    cx,
    cy,
    left_ref,
    rows_ref,
    next_x_ref,
    last_x_ref,
    next_y_ref,
    last_y_ref,
    entries_ref,
    present_ref,
    owners_ref,
    targets_ref,
    out_ref,
    sums_ref,
    wide_ref,
    count_ref,
):
    count = cx * cy
    sums_ref[...] = jnp.zeros_like(sums_ref)

    def add(block, users):
        stack = [left_ref[x * cy + y, d] for x, y, d in users]
        stack = stack[0] if len(stack) == 1 else jnp.concatenate(stack, axis=0)
        terms = jnp.dot(stack, block, preferred_element_type=jnp.float32)
        for n, (x, y, d) in enumerate(users):
            entry = entries_ref[d, x, y]
            if d:
                entry = jnp.where(present_ref[x, d - 1, y] != 0, entry, count)
            sums_ref[entry] = sums_ref[entry] + terms[n * 64 : n * 64 + 64]

    for x in range(cx):
        for y in range(cy):
            users = [(x, y, 0), (x - 1, y, 1), (x + 1, y, 2), (x, y - 1, 3), (x, y + 1, 4)]
            users = [u for u in users if 0 <= u[0] < cx and 0 <= u[1] < cy]
            add(rows_ref[x * cy + y], users)
    for y in range(cy):
        add(unpacked(next_x_ref[y], wide_ref.at[y % 4]), [(cx - 1, y, 1)])
    for y in range(cy):
        add(unpacked(last_x_ref[y], wide_ref.at[y % 4]), [(0, y, 2)])
    for x in range(cx):
        add(unpacked(next_y_ref[x], wide_ref.at[x % 4]), [(x, cy - 1, 3)])
    for x in range(cx):
        add(unpacked(last_y_ref[x], wide_ref.at[x % 4]), [(x, 0, 4)])

    for ring in range(RING):
        count_ref[ring] = 0
    row_id = lax.broadcasted_iota(jnp.int32, (RING, 128), 0)
    lane_id = lax.broadcasted_iota(jnp.int32, (RING, 128), 1)
    low = lax.broadcasted_iota(jnp.int32, (32, 128), 1) < 64
    tags = jnp.full((RING, 128), 1.0, jnp.float32) * (RING * SLOTS)
    for e in range(count):
        owner = owners_ref[e]
        ring = owner % RING
        slot = count_ref[ring]
        count_ref[ring] = slot + 1
        even = sums_ref[e, pl.ds(0, 32, stride=2), :]
        odd = sums_ref[e, pl.ds(1, 32, stride=2), :]
        block = jnp.where(low, even, pltpu.roll(odd, 64, 1)).astype(jnp.bfloat16)
        out_ref[ring, pl.ds(pl.multiple_of(slot * 32, 32), 32), :] = block
        tag = (owner // RING) * 16 + targets_ref[e]
        tags = jnp.where((row_id == ring) & (lane_id == slot), tag.astype(jnp.float32), tags)
    for ring in range(RING):
        row = jnp.broadcast_to(tags[ring : ring + 1, :], (16, 128))
        out_ref[ring, SLOTS * 32 : SLOTS * 32 + 16, :] = row.astype(jnp.bfloat16)


def gather_kernel(blocks, got_ref, tags_ref, out_ref, sums_ref):
    sums_ref[...] = jnp.zeros_like(sums_ref)
    for ring in range(RING):
        for slot in range(SLOTS):
            tag = jnp.minimum(tags_ref[ring, slot], blocks)
            piece = got_ref[ring, slot * 32 : slot * 32 + 32, :].astype(jnp.float32)
            sums_ref[tag] = sums_ref[tag] + piece
    out_ref[...] = sums_ref[:blocks].astype(jnp.bfloat16)


def shards(couplings, prolong, present, entries, owners, targets):
    cx, cy = prolong.shape[0], prolong.shape[1]
    cells = cx * cy
    nx, ny = lax.axis_size("gx"), lax.axis_size("gy")
    across = ny // RING
    along = [[x * RING + z for z in range(RING)] for x in range(across)]
    aside = [[x * RING + z for x in range(across)] for z in range(RING)]
    owned = 16

    up_x = [(i, i + 1) for i in range(nx - 1)]
    down_x = [(i + 1, i) for i in range(nx - 1)]
    up_y = [(i, i + 1) for i in range(ny - 1)]
    down_y = [(i + 1, i) for i in range(ny - 1)]
    next_y = lax.ppermute(prolong[:, 0], "gy", down_y)
    last_y = lax.ppermute(prolong[:, cy - 1], "gy", up_y)
    next_x = lax.ppermute(prolong[0], "gx", down_x)
    last_x = lax.ppermute(prolong[cx - 1], "gx", up_x)

    left, rows = pl.pallas_call(
        left_kernel,
        out_shape=(
            jax.ShapeDtypeStruct((cells, 5, 64, 64), jnp.bfloat16),
            jax.ShapeDtypeStruct((cells, 64, 128), jnp.bfloat16),
        ),
        in_specs=[VMEM, VMEM],
        out_specs=(VMEM, VMEM),
        scratch_shapes=[pltpu.VMEM((4, 64, 128), jnp.float32)],
        compiler_params=PARAMS,
        cost_estimate=pl.CostEstimate(
            flops=cells * 5 * 2 * 64**3 * 8, bytes_accessed=cells * 90000, transcendentals=0
        ),
        name="left_factor",
    )(prolong.reshape(cells, 32, 128), couplings.reshape(cells, 64, 320))

    outgoing = pl.pallas_call(
        lambda *refs: partial_kernel(cx, cy, *refs),
        out_shape=jax.ShapeDtypeStruct((RING, SLOTS * 32 + 16, 128), jnp.bfloat16),
        in_specs=[VMEM] * 6 + [SMEM] * 4,
        out_specs=VMEM,
        scratch_shapes=[
            pltpu.VMEM((cells + 1, 64, 128), jnp.float32),
            pltpu.VMEM((4, 64, 128), jnp.float32),
            pltpu.SMEM((RING,), jnp.int32),
        ],
        compiler_params=PARAMS,
        name="partial_blocks",
    )(
        left,
        rows,
        next_x,
        last_x,
        next_y,
        last_y,
        jnp.transpose(entries, (2, 0, 1)),
        jnp.transpose(present, (0, 2, 1)),
        owners.reshape(cells),
        targets.reshape(cells),
    )
    got = lax.all_to_all(outgoing, "gy", 0, 0, axis_index_groups=along, tiled=True)
    tags = got[:, SLOTS * 32, :SLOTS].astype(jnp.int32)
    blocks = across * owned
    dense = pl.pallas_call(
        lambda *refs: gather_kernel(blocks, *refs),
        out_shape=jax.ShapeDtypeStruct((blocks, 32, 128), jnp.bfloat16),
        in_specs=[VMEM, SMEM],
        out_specs=VMEM,
        scratch_shapes=[pltpu.VMEM((blocks + 1, 32, 128), jnp.float32)],
        compiler_params=PARAMS,
        name="ring_sums",
    )(got, tags)
    pieces = lax.all_to_all(
        dense.reshape(across, owned * 32, 128), "gy", 0, 0, axis_index_groups=aside, tiled=True
    )
    coarse = jnp.sum(pieces.astype(jnp.float32), axis=0).astype(jnp.bfloat16)
    return coarse.reshape(1, owned, 32, 128)


def solution(mesh):
    in_specs = (
        P("gx", "gy", None, None),
        P("gx", "gy", None, None),
        P("gx", "gy", None),
        P("gx", "gy", None),
        P("gx", "gy", None),
        P("gx", "gy"),
    )
    out_specs = P("gx", "gy", None, None)
    return jax.shard_map(shards, mesh=mesh, in_specs=in_specs, out_specs=out_specs, check_vma=False)
```

```python
import jax
import jax.numpy as jnp
from jax import lax
from jax.experimental import pallas as pl
from jax.experimental.pallas import tpu as pltpu
from jax.sharding import PartitionSpec as P

RING = 16
SLOTS = 8
FIRST = 4
VMEM = pl.BlockSpec(memory_space=pltpu.VMEM)
SMEM = pl.BlockSpec(memory_space=pltpu.SMEM)
PARAMS = pltpu.CompilerParams(vmem_limit_bytes=40 * 1024 * 1024)


def unpacked(lines, wide_ref):
    lines = lines.astype(jnp.float32)
    wide_ref[pl.ds(0, 32, stride=2), :] = lines
    wide_ref[pl.ds(1, 32, stride=2), :] = pltpu.roll(lines, 64, 1)
    return wide_ref[...].astype(jnp.bfloat16)


def left_kernel(prolong_ref, couplings_ref, left_ref, rows_ref, wide_ref):
    for cell in range(prolong_ref.shape[0]):
        rows = unpacked(prolong_ref[cell], wide_ref.at[cell % 4])
        rows_ref[cell] = rows
        product = lax.dot_general(
            rows[:, :64],
            couplings_ref[cell],
            (((0,), (0,)), ((), ())),
            preferred_element_type=jnp.float32,
        ).astype(jnp.bfloat16)
        for d in range(5):
            left_ref[cell, d] = product[:, d * 64 : d * 64 + 64]


def partial_kernel(
    cx,
    cy,
    left_ref,
    rows_ref,
    next_x_ref,
    last_x_ref,
    next_y_ref,
    last_y_ref,
    entries_ref,
    present_ref,
    owners_ref,
    targets_ref,
    out_ref,
    late_ref,
    sums_ref,
    wide_ref,
    count_ref,
):
    count = cx * cy
    sums_ref[...] = jnp.zeros_like(sums_ref)

    def add(block, users):
        stack = [left_ref[x * cy + y, d] for x, y, d in users]
        stack = stack[0] if len(stack) == 1 else jnp.concatenate(stack, axis=0)
        terms = jnp.dot(stack, block, preferred_element_type=jnp.float32)
        for n, (x, y, d) in enumerate(users):
            entry = entries_ref[d, x, y]
            if d:
                entry = jnp.where(present_ref[x, d - 1, y] != 0, entry, count)
            sums_ref[entry] = sums_ref[entry] + terms[n * 64 : n * 64 + 64]

    for x in range(cx):
        for y in range(cy):
            users = [(x, y, 0), (x - 1, y, 1), (x + 1, y, 2), (x, y - 1, 3), (x, y + 1, 4)]
            users = [u for u in users if 0 <= u[0] < cx and 0 <= u[1] < cy]
            add(rows_ref[x * cy + y], users)
    for y in range(cy):
        add(unpacked(next_x_ref[y], wide_ref.at[y % 4]), [(cx - 1, y, 1)])
    for y in range(cy):
        add(unpacked(last_x_ref[y], wide_ref.at[y % 4]), [(0, y, 2)])
    for x in range(cx):
        add(unpacked(next_y_ref[x], wide_ref.at[x % 4]), [(x, cy - 1, 3)])
    for x in range(cx):
        add(unpacked(last_y_ref[x], wide_ref.at[x % 4]), [(x, 0, 4)])

    for ring in range(RING):
        count_ref[ring] = 0
    row_id = lax.broadcasted_iota(jnp.int32, (RING, 128), 0)
    lane_id = lax.broadcasted_iota(jnp.int32, (RING, 128), 1)
    low = lax.broadcasted_iota(jnp.int32, (32, 128), 1) < 64
    tags = jnp.full((RING, 128), 128.0, jnp.float32)
    most = jnp.int32(0)
    for e in range(count):
        owner = owners_ref[e]
        ring = owner % RING
        slot = count_ref[ring]
        count_ref[ring] = slot + 1
        even = sums_ref[e, pl.ds(0, 32, stride=2), :]
        odd = sums_ref[e, pl.ds(1, 32, stride=2), :]
        block = jnp.where(low, even, pltpu.roll(odd, 64, 1)).astype(jnp.bfloat16)
        most = jnp.maximum(most, slot)

        @pl.when(slot < FIRST)
        def _():
            out_ref[ring, pl.ds(pl.multiple_of(slot * 32, 32), 32), :] = block

        @pl.when(slot >= FIRST)
        def _():
            late_ref[ring, pl.ds(pl.multiple_of((slot - FIRST) * 32, 32), 32), :] = block

        tag = (owner // RING) * 16 + targets_ref[e]
        tags = jnp.where((row_id == ring) & (lane_id == slot), tag.astype(jnp.float32), tags)
    late = (most >= FIRST).astype(jnp.float32)
    tags = jnp.where(lane_id == SLOTS, late, tags)
    for ring in range(RING):
        row = jnp.broadcast_to(tags[ring : ring + 1, :], (16, 128))
        out_ref[ring, FIRST * 32 : FIRST * 32 + 16, :] = row.astype(jnp.bfloat16)


def gather_kernel(blocks, got_ref, late_ref, tags_ref, any_ref, out_ref, sums_ref):
    sums_ref[...] = jnp.zeros_like(sums_ref)

    def add(ring, slot, from_ref, place):
        tag = jnp.minimum(tags_ref[ring, slot], blocks)
        piece = from_ref[ring, place * 32 : place * 32 + 32, :].astype(jnp.float32)
        sums_ref[tag] = sums_ref[tag] + piece

    for ring in range(RING):
        for slot in range(FIRST):
            add(ring, slot, got_ref, slot)

    @pl.when(any_ref[0] != 0)
    def _():
        for ring in range(RING):
            for slot in range(FIRST, SLOTS):
                add(ring, slot, late_ref, slot - FIRST)

    out_ref[...] = sums_ref[:blocks].astype(jnp.bfloat16)


def shards(couplings, prolong, present, entries, owners, targets):
    cx, cy = prolong.shape[0], prolong.shape[1]
    cells = cx * cy
    nx, ny = lax.axis_size("gx"), lax.axis_size("gy")
    across = ny // RING
    along = [[x * RING + z for z in range(RING)] for x in range(across)]
    aside = [[x * RING + z for x in range(across)] for z in range(RING)]
    owned = 16

    up_x = [(i, i + 1) for i in range(nx - 1)]
    down_x = [(i + 1, i) for i in range(nx - 1)]
    up_y = [(i, i + 1) for i in range(ny - 1)]
    down_y = [(i + 1, i) for i in range(ny - 1)]
    next_y = lax.ppermute(prolong[:, 0], "gy", down_y)
    last_y = lax.ppermute(prolong[:, cy - 1], "gy", up_y)
    next_x = lax.ppermute(prolong[0], "gx", down_x)
    last_x = lax.ppermute(prolong[cx - 1], "gx", up_x)

    left, rows = pl.pallas_call(
        left_kernel,
        out_shape=(
            jax.ShapeDtypeStruct((cells, 5, 64, 64), jnp.bfloat16),
            jax.ShapeDtypeStruct((cells, 64, 128), jnp.bfloat16),
        ),
        in_specs=[VMEM, VMEM],
        out_specs=(VMEM, VMEM),
        scratch_shapes=[pltpu.VMEM((4, 64, 128), jnp.float32)],
        compiler_params=PARAMS,
        cost_estimate=pl.CostEstimate(
            flops=cells * 5 * 2 * 64**3 * 8, bytes_accessed=cells * 90000, transcendentals=0
        ),
        name="left_factor",
    )(prolong.reshape(cells, 32, 128), couplings.reshape(cells, 64, 320))

    outgoing, outgoing_late = pl.pallas_call(
        lambda *refs: partial_kernel(cx, cy, *refs),
        out_shape=(
            jax.ShapeDtypeStruct((RING, FIRST * 32 + 16, 128), jnp.bfloat16),
            jax.ShapeDtypeStruct((RING, (SLOTS - FIRST) * 32, 128), jnp.bfloat16),
        ),
        in_specs=[VMEM] * 6 + [SMEM] * 4,
        out_specs=(VMEM, VMEM),
        scratch_shapes=[
            pltpu.VMEM((cells + 1, 64, 128), jnp.float32),
            pltpu.VMEM((4, 64, 128), jnp.float32),
            pltpu.SMEM((RING,), jnp.int32),
        ],
        compiler_params=PARAMS,
        name="partial_blocks",
    )(
        left,
        rows,
        next_x,
        last_x,
        next_y,
        last_y,
        jnp.transpose(entries, (2, 0, 1)),
        jnp.transpose(present, (0, 2, 1)),
        owners.reshape(cells),
        targets.reshape(cells),
    )

    def exchange(array):
        return lax.all_to_all(array, "gy", 0, 0, axis_index_groups=along, tiled=True)

    got = exchange(outgoing)
    heads = got[:, FIRST * 32, : SLOTS + 1].astype(jnp.int32)
    tags = heads[:, :SLOTS]
    any_late = jnp.max(heads[:, SLOTS])
    got_late = lax.cond(any_late > 0, exchange, lambda array: array, outgoing_late)
    blocks = across * owned
    dense = pl.pallas_call(
        lambda *refs: gather_kernel(blocks, *refs),
        out_shape=jax.ShapeDtypeStruct((blocks, 32, 128), jnp.bfloat16),
        in_specs=[VMEM, VMEM, SMEM, SMEM],
        out_specs=VMEM,
        scratch_shapes=[pltpu.VMEM((blocks + 1, 32, 128), jnp.float32)],
        compiler_params=PARAMS,
        name="ring_sums",
    )(got, got_late, tags, any_late.reshape(1))
    pieces = lax.all_to_all(
        dense.reshape(across, owned * 32, 128), "gy", 0, 0, axis_index_groups=aside, tiled=True
    )
    coarse = jnp.sum(pieces.astype(jnp.float32), axis=0).astype(jnp.bfloat16)
    return coarse.reshape(1, owned, 32, 128)


def solution(mesh):
    in_specs = (
        P("gx", "gy", None, None),
        P("gx", "gy", None, None),
        P("gx", "gy", None),
        P("gx", "gy", None),
        P("gx", "gy", None),
        P("gx", "gy"),
    )
    out_specs = P("gx", "gy", None, None)
    return jax.shard_map(shards, mesh=mesh, in_specs=in_specs, out_specs=out_specs, check_vma=False)
```

```python
import jax
import jax.numpy as jnp
from jax import lax
from jax.experimental import pallas as pl
from jax.experimental.pallas import tpu as pltpu
from jax.sharding import PartitionSpec as P

RING = 16
SLOTS = 8
FIRST = 6
VMEM = pl.BlockSpec(memory_space=pltpu.VMEM)
SMEM = pl.BlockSpec(memory_space=pltpu.SMEM)
PARAMS = pltpu.CompilerParams(vmem_limit_bytes=40 * 1024 * 1024)


def unpacked(lines, wide_ref):
    lines = lines.astype(jnp.float32)
    wide_ref[pl.ds(0, 32, stride=2), :] = lines
    wide_ref[pl.ds(1, 32, stride=2), :] = pltpu.roll(lines, 64, 1)
    return wide_ref[...].astype(jnp.bfloat16)


def left_kernel(prolong_ref, couplings_ref, left_ref, rows_ref, wide_ref):
    for cell in range(prolong_ref.shape[0]):
        rows = unpacked(prolong_ref[cell], wide_ref.at[cell % 4])
        rows_ref[cell] = rows
        product = lax.dot_general(
            rows[:, :64],
            couplings_ref[cell],
            (((0,), (0,)), ((), ())),
            preferred_element_type=jnp.float32,
        ).astype(jnp.bfloat16)
        for d in range(5):
            left_ref[cell, d] = product[:, d * 64 : d * 64 + 64]


def partial_kernel(
    cx,
    cy,
    left_ref,
    rows_ref,
    next_x_ref,
    last_x_ref,
    next_y_ref,
    last_y_ref,
    entries_ref,
    present_ref,
    owners_ref,
    targets_ref,
    out_ref,
    late_ref,
    sums_ref,
    wide_ref,
    count_ref,
):
    count = cx * cy
    sums_ref[...] = jnp.zeros_like(sums_ref)

    def add(block, users):
        stack = [left_ref[x * cy + y, d] for x, y, d in users]
        stack = stack[0] if len(stack) == 1 else jnp.concatenate(stack, axis=0)
        terms = jnp.dot(stack, block, preferred_element_type=jnp.float32)
        for n, (x, y, d) in enumerate(users):
            entry = entries_ref[d, x, y]
            if d:
                entry = jnp.where(present_ref[x, d - 1, y] != 0, entry, count)
            sums_ref[entry] = sums_ref[entry] + terms[n * 64 : n * 64 + 64]

    for x in range(cx):
        for y in range(cy):
            users = [(x, y, 0), (x - 1, y, 1), (x + 1, y, 2), (x, y - 1, 3), (x, y + 1, 4)]
            users = [u for u in users if 0 <= u[0] < cx and 0 <= u[1] < cy]
            add(rows_ref[x * cy + y], users)
    for y in range(cy):
        add(unpacked(next_x_ref[y], wide_ref.at[y % 4]), [(cx - 1, y, 1)])
    for y in range(cy):
        add(unpacked(last_x_ref[y], wide_ref.at[y % 4]), [(0, y, 2)])
    for x in range(cx):
        add(unpacked(next_y_ref[x], wide_ref.at[x % 4]), [(x, cy - 1, 3)])
    for x in range(cx):
        add(unpacked(last_y_ref[x], wide_ref.at[x % 4]), [(x, 0, 4)])

    for ring in range(RING):
        count_ref[ring] = 0
    row_id = lax.broadcasted_iota(jnp.int32, (RING, 128), 0)
    lane_id = lax.broadcasted_iota(jnp.int32, (RING, 128), 1)
    low = lax.broadcasted_iota(jnp.int32, (32, 128), 1) < 64
    tags = jnp.full((RING, 128), 128.0, jnp.float32)
    most = jnp.int32(0)
    for e in range(count):
        owner = owners_ref[e]
        ring = owner % RING
        slot = count_ref[ring]
        count_ref[ring] = slot + 1
        even = sums_ref[e, pl.ds(0, 32, stride=2), :]
        odd = sums_ref[e, pl.ds(1, 32, stride=2), :]
        block = jnp.where(low, even, pltpu.roll(odd, 64, 1)).astype(jnp.bfloat16)
        most = jnp.maximum(most, slot)

        @pl.when(slot < FIRST)
        def _():
            out_ref[ring, pl.ds(pl.multiple_of(slot * 32, 32), 32), :] = block

        @pl.when(slot >= FIRST)
        def _():
            late_ref[ring, pl.ds(pl.multiple_of((slot - FIRST) * 32, 32), 32), :] = block

        tag = (owner // RING) * 16 + targets_ref[e]
        tags = jnp.where((row_id == ring) & (lane_id == slot), tag.astype(jnp.float32), tags)
    late = (most >= FIRST).astype(jnp.float32)
    tags = jnp.where(lane_id == SLOTS, late, tags)
    for ring in range(RING):
        row = jnp.broadcast_to(tags[ring : ring + 1, :], (16, 128))
        out_ref[ring, FIRST * 32 : FIRST * 32 + 16, :] = row.astype(jnp.bfloat16)


def gather_kernel(blocks, got_ref, late_ref, tags_ref, any_ref, out_ref, sums_ref):
    sums_ref[...] = jnp.zeros_like(sums_ref)

    def add(ring, slot, from_ref, place):
        tag = jnp.minimum(tags_ref[ring, slot], blocks)
        piece = from_ref[ring, place * 32 : place * 32 + 32, :].astype(jnp.float32)
        sums_ref[tag] = sums_ref[tag] + piece

    for ring in range(RING):
        for slot in range(FIRST):
            add(ring, slot, got_ref, slot)

    @pl.when(any_ref[0] != 0)
    def _():
        for ring in range(RING):
            for slot in range(FIRST, SLOTS):
                add(ring, slot, late_ref, slot - FIRST)

    out_ref[...] = sums_ref[:blocks].astype(jnp.bfloat16)


def shards(couplings, prolong, present, entries, owners, targets):
    cx, cy = prolong.shape[0], prolong.shape[1]
    cells = cx * cy
    nx, ny = lax.axis_size("gx"), lax.axis_size("gy")
    across = ny // RING
    along = [[x * RING + z for z in range(RING)] for x in range(across)]
    aside = [[x * RING + z for x in range(across)] for z in range(RING)]
    owned = 16

    up_x = [(i, i + 1) for i in range(nx - 1)]
    down_x = [(i + 1, i) for i in range(nx - 1)]
    up_y = [(i, i + 1) for i in range(ny - 1)]
    down_y = [(i + 1, i) for i in range(ny - 1)]
    next_y = lax.ppermute(prolong[:, 0], "gy", down_y)
    last_y = lax.ppermute(prolong[:, cy - 1], "gy", up_y)
    next_x = lax.ppermute(prolong[0], "gx", down_x)
    last_x = lax.ppermute(prolong[cx - 1], "gx", up_x)

    left, rows = pl.pallas_call(
        left_kernel,
        out_shape=(
            jax.ShapeDtypeStruct((cells, 5, 64, 64), jnp.bfloat16),
            jax.ShapeDtypeStruct((cells, 64, 128), jnp.bfloat16),
        ),
        in_specs=[VMEM, VMEM],
        out_specs=(VMEM, VMEM),
        scratch_shapes=[pltpu.VMEM((4, 64, 128), jnp.float32)],
        compiler_params=PARAMS,
        cost_estimate=pl.CostEstimate(
            flops=cells * 5 * 2 * 64**3 * 8, bytes_accessed=cells * 90000, transcendentals=0
        ),
        name="left_factor",
    )(prolong.reshape(cells, 32, 128), couplings.reshape(cells, 64, 320))

    outgoing, outgoing_late = pl.pallas_call(
        lambda *refs: partial_kernel(cx, cy, *refs),
        out_shape=(
            jax.ShapeDtypeStruct((RING, FIRST * 32 + 16, 128), jnp.bfloat16),
            jax.ShapeDtypeStruct((RING, (SLOTS - FIRST) * 32, 128), jnp.bfloat16),
        ),
        in_specs=[VMEM] * 6 + [SMEM] * 4,
        out_specs=(VMEM, VMEM),
        scratch_shapes=[
            pltpu.VMEM((cells + 1, 64, 128), jnp.float32),
            pltpu.VMEM((4, 64, 128), jnp.float32),
            pltpu.SMEM((RING,), jnp.int32),
        ],
        compiler_params=PARAMS,
        name="partial_blocks",
    )(
        left,
        rows,
        next_x,
        last_x,
        next_y,
        last_y,
        jnp.transpose(entries, (2, 0, 1)),
        jnp.transpose(present, (0, 2, 1)),
        owners.reshape(cells),
        targets.reshape(cells),
    )

    def exchange(array):
        return lax.all_to_all(array, "gy", 0, 0, axis_index_groups=along, tiled=True)

    got = exchange(outgoing)
    heads = got[:, FIRST * 32, : SLOTS + 1].astype(jnp.int32)
    tags = heads[:, :SLOTS]
    any_late = jnp.max(heads[:, SLOTS])
    got_late = lax.cond(any_late > 0, exchange, lambda array: array, outgoing_late)
    blocks = across * owned
    dense = pl.pallas_call(
        lambda *refs: gather_kernel(blocks, *refs),
        out_shape=jax.ShapeDtypeStruct((blocks, 32, 128), jnp.bfloat16),
        in_specs=[VMEM, VMEM, SMEM, SMEM],
        out_specs=VMEM,
        scratch_shapes=[pltpu.VMEM((blocks + 1, 32, 128), jnp.float32)],
        compiler_params=PARAMS,
        name="ring_sums",
    )(got, got_late, tags, any_late.reshape(1))
    pieces = lax.all_to_all(
        dense.reshape(across, owned * 32, 128), "gy", 0, 0, axis_index_groups=aside, tiled=True
    )
    coarse = jnp.sum(pieces.astype(jnp.float32), axis=0).astype(jnp.bfloat16)
    return coarse.reshape(1, owned, 32, 128)


def solution(mesh):
    in_specs = (
        P("gx", "gy", None, None),
        P("gx", "gy", None, None),
        P("gx", "gy", None),
        P("gx", "gy", None),
        P("gx", "gy", None),
        P("gx", "gy"),
    )
    out_specs = P("gx", "gy", None, None)
    return jax.shard_map(shards, mesh=mesh, in_specs=in_specs, out_specs=out_specs, check_vma=False)
```

```python
import jax
import jax.numpy as jnp
from jax import lax
from jax.experimental import pallas as pl
from jax.experimental.pallas import tpu as pltpu
from jax.sharding import PartitionSpec as P

RING = 16
SLOTS = 8
FIRST = 6
VMEM = pl.BlockSpec(memory_space=pltpu.VMEM)
SMEM = pl.BlockSpec(memory_space=pltpu.SMEM)
PARAMS = pltpu.CompilerParams(vmem_limit_bytes=40 * 1024 * 1024)


def unpacked(lines, wide_ref):
    lines = lines.astype(jnp.float32)
    wide_ref[pl.ds(0, 32, stride=2), :] = lines
    wide_ref[pl.ds(1, 32, stride=2), :] = pltpu.roll(lines, 64, 1)
    return wide_ref[...].astype(jnp.bfloat16)


def left_kernel(prolong_ref, couplings_ref, left_ref, rows_ref, wide_ref):
    for cell in range(prolong_ref.shape[0]):
        rows = unpacked(prolong_ref[cell], wide_ref.at[cell % 4])
        rows_ref[cell] = rows
        product = lax.dot_general(
            rows[:, :64],
            couplings_ref[cell],
            (((0,), (0,)), ((), ())),
            preferred_element_type=jnp.float32,
        ).astype(jnp.bfloat16)
        for d in range(5):
            left_ref[cell, d] = product[:, d * 64 : d * 64 + 64]


def partial_kernel(
    cx,
    cy,
    left_ref,
    rows_ref,
    next_x_ref,
    last_x_ref,
    next_y_ref,
    last_y_ref,
    entries_ref,
    present_ref,
    owners_ref,
    targets_ref,
    place_ref,
    *rest,
):
    out_refs, (late_ref, sums_ref, wide_ref, slots_ref, count_ref) = rest[:RING], rest[RING:]
    count = cx * cy
    sums_ref[...] = jnp.zeros_like(sums_ref)

    def add(block, users):
        stack = [left_ref[x * cy + y, d] for x, y, d in users]
        stack = stack[0] if len(stack) == 1 else jnp.concatenate(stack, axis=0)
        terms = jnp.dot(stack, block, preferred_element_type=jnp.float32)
        for n, (x, y, d) in enumerate(users):
            entry = entries_ref[d, x, y]
            if d:
                entry = jnp.where(present_ref[x, d - 1, y] != 0, entry, count)
            sums_ref[entry] = sums_ref[entry] + terms[n * 64 : n * 64 + 64]

    for x in range(cx):
        for y in range(cy):
            users = [(x, y, 0), (x - 1, y, 1), (x + 1, y, 2), (x, y - 1, 3), (x, y + 1, 4)]
            users = [u for u in users if 0 <= u[0] < cx and 0 <= u[1] < cy]
            add(rows_ref[x * cy + y], users)
    for y in range(cy):
        add(unpacked(next_x_ref[y], wide_ref.at[y % 4]), [(cx - 1, y, 1)])
    for y in range(cy):
        add(unpacked(last_x_ref[y], wide_ref.at[y % 4]), [(0, y, 2)])
    for x in range(cx):
        add(unpacked(next_y_ref[x], wide_ref.at[x % 4]), [(x, cy - 1, 3)])
    for x in range(cx):
        add(unpacked(last_y_ref[x], wide_ref.at[x % 4]), [(x, 0, 4)])

    place = place_ref[0]
    for ring in range(RING):
        count_ref[ring] = 0
    row_id = lax.broadcasted_iota(jnp.int32, (RING, 128), 0)
    lane_id = lax.broadcasted_iota(jnp.int32, (RING, 128), 1)
    low = lax.broadcasted_iota(jnp.int32, (32, 128), 1) < 64
    tags = jnp.full((RING, 128), 128.0, jnp.float32)
    most = jnp.int32(0)
    for e in range(count):
        owner = owners_ref[e]
        ring = (owner - place + RING) % RING
        slot = count_ref[ring]
        count_ref[ring] = slot + 1
        even = sums_ref[e, pl.ds(0, 32, stride=2), :]
        odd = sums_ref[e, pl.ds(1, 32, stride=2), :]
        block = jnp.where(low, even, pltpu.roll(odd, 64, 1)).astype(jnp.bfloat16)
        most = jnp.maximum(most, slot)

        slots_ref[ring, pl.ds(pl.multiple_of(slot * 32, 32), 32), :] = block
        tag = (owner // RING) * 16 + targets_ref[e]
        tags = jnp.where((row_id == ring) & (lane_id == slot), tag.astype(jnp.float32), tags)
    late = (most >= FIRST).astype(jnp.float32)
    tags = jnp.where(lane_id == SLOTS, late, tags)
    for ring in range(RING):
        row = jnp.broadcast_to(tags[ring : ring + 1, :], (16, 128))
        out_refs[ring][: FIRST * 32, :] = slots_ref[ring, : FIRST * 32, :]
        out_refs[ring][FIRST * 32 :, :] = row.astype(jnp.bfloat16)
        late_ref[(ring + place) % RING] = slots_ref[ring, FIRST * 32 :, :]


def gather_kernel(blocks, place_ref, tags_ref, any_ref, late_ref, *rest):
    got_refs, (out_ref, sums_ref) = rest[:RING], rest[RING:]
    sums_ref[...] = jnp.zeros_like(sums_ref)

    def add(tag, piece):
        tag = jnp.minimum(tag, blocks)
        sums_ref[tag] = sums_ref[tag] + piece.astype(jnp.float32)

    for ring in range(RING):
        for slot in range(FIRST):
            add(tags_ref[ring, slot], got_refs[ring][slot * 32 : slot * 32 + 32, :])

    @pl.when(any_ref[0] != 0)
    def _():
        for source in range(RING):
            ring = (place_ref[0] - source + RING) % RING
            for slot in range(FIRST, SLOTS):
                start = (slot - FIRST) * 32
                add(tags_ref[ring, slot], late_ref[source, start : start + 32, :])

    out_ref[...] = sums_ref[:blocks].astype(jnp.bfloat16)


def shards(couplings, prolong, present, entries, owners, targets):
    cx, cy = prolong.shape[0], prolong.shape[1]
    cells = cx * cy
    nx, ny = lax.axis_size("gx"), lax.axis_size("gy")
    across = ny // RING
    along = [[x * RING + z for z in range(RING)] for x in range(across)]
    aside = [[x * RING + z for x in range(across)] for z in range(RING)]
    owned = 16

    up_x = [(i, i + 1) for i in range(nx - 1)]
    down_x = [(i + 1, i) for i in range(nx - 1)]
    up_y = [(i, i + 1) for i in range(ny - 1)]
    down_y = [(i + 1, i) for i in range(ny - 1)]
    next_y = lax.ppermute(prolong[:, 0], "gy", down_y)
    last_y = lax.ppermute(prolong[:, cy - 1], "gy", up_y)
    next_x = lax.ppermute(prolong[0], "gx", down_x)
    last_x = lax.ppermute(prolong[cx - 1], "gx", up_x)

    left, rows = pl.pallas_call(
        left_kernel,
        out_shape=(
            jax.ShapeDtypeStruct((cells, 5, 64, 64), jnp.bfloat16),
            jax.ShapeDtypeStruct((cells, 64, 128), jnp.bfloat16),
        ),
        in_specs=[VMEM, VMEM],
        out_specs=(VMEM, VMEM),
        scratch_shapes=[pltpu.VMEM((4, 64, 128), jnp.float32)],
        compiler_params=PARAMS,
        cost_estimate=pl.CostEstimate(
            flops=cells * 5 * 2 * 64**3 * 8, bytes_accessed=cells * 90000, transcendentals=0
        ),
        name="left_factor",
    )(prolong.reshape(cells, 32, 128), couplings.reshape(cells, 64, 320))

    place = (lax.axis_index("gy") % RING).astype(jnp.int32).reshape(1)
    *outgoing, outgoing_late = pl.pallas_call(
        lambda *refs: partial_kernel(cx, cy, *refs),
        out_shape=(jax.ShapeDtypeStruct((FIRST * 32 + 16, 128), jnp.bfloat16),) * RING
        + (jax.ShapeDtypeStruct((RING, (SLOTS - FIRST) * 32, 128), jnp.bfloat16),),
        in_specs=[VMEM] * 6 + [SMEM] * 5,
        out_specs=(VMEM,) * (RING + 1),
        scratch_shapes=[
            pltpu.VMEM((cells + 1, 64, 128), jnp.float32),
            pltpu.VMEM((4, 64, 128), jnp.float32),
            pltpu.VMEM((RING, SLOTS * 32, 128), jnp.bfloat16),
            pltpu.SMEM((RING,), jnp.int32),
        ],
        compiler_params=PARAMS,
        name="partial_blocks",
    )(
        left,
        rows,
        next_x,
        last_x,
        next_y,
        last_y,
        jnp.transpose(entries, (2, 0, 1)),
        jnp.transpose(present, (0, 2, 1)),
        owners.reshape(cells),
        targets.reshape(cells),
        place,
    )

    got = [outgoing[0]] + [None] * (RING - 1)
    for step in sorted(range(1, RING), key=lambda n: -min(n, RING - n)):
        pairs = [(ring[z], ring[(z + step) % RING]) for ring in along for z in range(RING)]
        got[step] = lax.ppermute(outgoing[step], "gy", pairs)
    heads = jnp.stack([g[FIRST * 32, : SLOTS + 1] for g in got]).astype(jnp.int32)
    tags = heads[:, :SLOTS]
    any_late = jnp.max(heads[:, SLOTS])
    got_late = lax.cond(
        any_late > 0,
        lambda array: lax.all_to_all(array, "gy", 0, 0, axis_index_groups=along, tiled=True),
        lambda array: array,
        outgoing_late,
    )
    blocks = across * owned
    dense = pl.pallas_call(
        lambda *refs: gather_kernel(blocks, *refs),
        out_shape=jax.ShapeDtypeStruct((blocks, 32, 128), jnp.bfloat16),
        in_specs=[SMEM] * 3 + [VMEM] * (RING + 1),
        out_specs=VMEM,
        scratch_shapes=[pltpu.VMEM((blocks + 1, 32, 128), jnp.float32)],
        compiler_params=PARAMS,
        name="ring_sums",
    )(place, tags, any_late.reshape(1), got_late, *got)
    pieces = lax.all_to_all(
        dense.reshape(across, owned * 32, 128), "gy", 0, 0, axis_index_groups=aside, tiled=True
    )
    coarse = jnp.sum(pieces.astype(jnp.float32), axis=0).astype(jnp.bfloat16)
    return coarse.reshape(1, owned, 32, 128)


def solution(mesh):
    in_specs = (
        P("gx", "gy", None, None),
        P("gx", "gy", None, None),
        P("gx", "gy", None),
        P("gx", "gy", None),
        P("gx", "gy", None),
        P("gx", "gy"),
    )
    out_specs = P("gx", "gy", None, None)
    return jax.shard_map(shards, mesh=mesh, in_specs=in_specs, out_specs=out_specs, check_vma=False)
```

```python
import jax
import jax.numpy as jnp
from jax import lax
from jax.experimental import pallas as pl
from jax.experimental.pallas import tpu as pltpu
from jax.sharding import PartitionSpec as P

RING = 16
SLOTS = 8
FIRST = 6
VMEM = pl.BlockSpec(memory_space=pltpu.VMEM)
SMEM = pl.BlockSpec(memory_space=pltpu.SMEM)
PARAMS = pltpu.CompilerParams(vmem_limit_bytes=40 * 1024 * 1024)


def unpacked(lines, wide_ref):
    lines = lines.astype(jnp.float32)
    wide_ref[pl.ds(0, 32, stride=2), :] = lines
    wide_ref[pl.ds(1, 32, stride=2), :] = pltpu.roll(lines, 64, 1)
    return wide_ref[...].astype(jnp.bfloat16)


def left_kernel(prolong_ref, couplings_ref, left_ref, rows_ref, wide_ref):
    for cell in range(prolong_ref.shape[0]):
        rows = unpacked(prolong_ref[cell], wide_ref.at[cell % 4])
        rows_ref[cell] = rows
        product = lax.dot_general(
            rows[:, :64],
            couplings_ref[cell],
            (((0,), (0,)), ((), ())),
            preferred_element_type=jnp.float32,
        ).astype(jnp.bfloat16)
        for d in range(5):
            left_ref[cell, d] = product[:, d * 64 : d * 64 + 64]


def partial_kernel(
    cx,
    cy,
    left_ref,
    rows_ref,
    near_x_ref,
    far_x_ref,
    near_y_ref,
    far_y_ref,
    entries_ref,
    present_ref,
    owners_ref,
    targets_ref,
    out_ref,
    late_ref,
    sums_ref,
    wide_ref,
    slots_ref,
    count_ref,
):
    count = cx * cy
    sums_ref[...] = jnp.zeros_like(sums_ref)

    def add(block, users):
        stack = [left_ref[x * cy + y, d] for x, y, d in users]
        stack = stack[0] if len(stack) == 1 else jnp.concatenate(stack, axis=0)
        terms = jnp.dot(stack, block, preferred_element_type=jnp.float32)
        for n, (x, y, d) in enumerate(users):
            entry = entries_ref[d, x, y]
            if not isinstance(d, int) or d > 0:
                entry = jnp.where(present_ref[x, d - 1, y] != 0, entry, count)
            sums_ref[entry] = sums_ref[entry] + terms[n * 64 : n * 64 + 64]

    for x in range(cx):
        for y in range(cy):
            users = [(x, y, 0), (x - 1, y, 1), (x + 1, y, 2), (x, y - 1, 3), (x, y + 1, 4)]
            users = [u for u in users if 0 <= u[0] < cx and 0 <= u[1] < cy]
            add(rows_ref[x * cy + y], users)
    for axis, far, block_ref in (
        ("gx", 0, near_x_ref),
        ("gx", 1, far_x_ref),
        ("gy", 0, near_y_ref),
        ("gy", 1, far_y_ref),
    ):
        is_next = lax.axis_index(axis) % 2 == far
        for n in range(cy if axis == "gx" else cx):
            block = unpacked(block_ref[n], wide_ref.at[n % 4])
            if axis == "gx":
                user = (jnp.where(is_next, cx - 1, 0), n, jnp.where(is_next, 1, 2))
            else:
                user = (n, jnp.where(is_next, cy - 1, 0), jnp.where(is_next, 3, 4))
            add(block, [user])

    for ring in range(RING):
        count_ref[ring] = 0
    row_id = lax.broadcasted_iota(jnp.int32, (RING, 128), 0)
    lane_id = lax.broadcasted_iota(jnp.int32, (RING, 128), 1)
    low = lax.broadcasted_iota(jnp.int32, (32, 128), 1) < 64
    tags = jnp.full((RING, 128), 128.0, jnp.float32)
    most = jnp.int32(0)
    for e in range(count):
        owner = owners_ref[e]
        ring = owner % RING
        slot = count_ref[ring]
        count_ref[ring] = slot + 1
        even = sums_ref[e, pl.ds(0, 32, stride=2), :]
        odd = sums_ref[e, pl.ds(1, 32, stride=2), :]
        block = jnp.where(low, even, pltpu.roll(odd, 64, 1)).astype(jnp.bfloat16)
        most = jnp.maximum(most, slot)

        slots_ref[ring, pl.ds(pl.multiple_of(slot * 32, 32), 32), :] = block
        tag = (owner // RING) * 16 + targets_ref[e]
        tags = jnp.where((row_id == ring) & (lane_id == slot), tag.astype(jnp.float32), tags)
    late = (most >= FIRST).astype(jnp.float32)
    tags = jnp.where(lane_id == SLOTS, late, tags)
    out_ref[:, : FIRST * 32, :] = slots_ref[:, : FIRST * 32, :]
    late_ref[...] = slots_ref[:, FIRST * 32 :, :]
    for ring in range(RING):
        row = jnp.broadcast_to(tags[ring : ring + 1, :], (16, 128))
        out_ref[ring, FIRST * 32 : FIRST * 32 + 16, :] = row.astype(jnp.bfloat16)


def gather_kernel(blocks, got_ref, late_ref, tags_ref, any_ref, out_ref, sums_ref):
    sums_ref[...] = jnp.zeros_like(sums_ref)

    def add(ring, slot, from_ref, place):
        tag = jnp.minimum(tags_ref[ring, slot], blocks)
        piece = from_ref[ring, place * 32 : place * 32 + 32, :].astype(jnp.float32)
        sums_ref[tag] = sums_ref[tag] + piece

    for ring in range(RING):
        for slot in range(FIRST):
            add(ring, slot, got_ref, slot)

    @pl.when(any_ref[0] != 0)
    def _():
        for ring in range(RING):
            for slot in range(FIRST, SLOTS):
                add(ring, slot, late_ref, slot - FIRST)

    out_ref[...] = sums_ref[:blocks].astype(jnp.bfloat16)


def shards(couplings, prolong, present, entries, owners, targets):
    cx, cy = prolong.shape[0], prolong.shape[1]
    cells = cx * cy
    across = lax.axis_size("gy") // RING
    along = [[x * RING + z for z in range(RING)] for x in range(across)]
    aside = [[x * RING + z for x in range(across)] for z in range(RING)]
    owned = 16

    def swapped(head, tail, axis):
        size = lax.axis_size(axis)
        even = lax.axis_index(axis) % 2 == 0
        near = [(i, i ^ 1) for i in range(size)]
        far = [(i, i + 1) for i in range(1, size - 1, 2)]
        far = far + [(j, i) for i, j in far]
        return (
            lax.ppermute(jnp.where(even, tail, head), axis, near),
            lax.ppermute(jnp.where(even, head, tail), axis, far),
        )

    near_x, far_x = swapped(prolong[0], prolong[cx - 1], "gx")
    near_y, far_y = swapped(prolong[:, 0], prolong[:, cy - 1], "gy")

    left, rows = pl.pallas_call(
        left_kernel,
        out_shape=(
            jax.ShapeDtypeStruct((cells, 5, 64, 64), jnp.bfloat16),
            jax.ShapeDtypeStruct((cells, 64, 128), jnp.bfloat16),
        ),
        in_specs=[VMEM, VMEM],
        out_specs=(VMEM, VMEM),
        scratch_shapes=[pltpu.VMEM((4, 64, 128), jnp.float32)],
        compiler_params=PARAMS,
        cost_estimate=pl.CostEstimate(
            flops=cells * 5 * 2 * 64**3 * 8, bytes_accessed=cells * 90000, transcendentals=0
        ),
        name="left_factor",
    )(prolong.reshape(cells, 32, 128), couplings.reshape(cells, 64, 320))

    outgoing, outgoing_late = pl.pallas_call(
        lambda *refs: partial_kernel(cx, cy, *refs),
        out_shape=(
            jax.ShapeDtypeStruct((RING, FIRST * 32 + 16, 128), jnp.bfloat16),
            jax.ShapeDtypeStruct((RING, (SLOTS - FIRST) * 32, 128), jnp.bfloat16),
        ),
        in_specs=[VMEM] * 6 + [SMEM] * 4,
        out_specs=(VMEM, VMEM),
        scratch_shapes=[
            pltpu.VMEM((cells + 1, 64, 128), jnp.float32),
            pltpu.VMEM((4, 64, 128), jnp.float32),
            pltpu.VMEM((RING, SLOTS * 32, 128), jnp.bfloat16),
            pltpu.SMEM((RING,), jnp.int32),
        ],
        compiler_params=PARAMS,
        name="partial_blocks",
    )(
        left,
        rows,
        near_x,
        far_x,
        near_y,
        far_y,
        jnp.transpose(entries, (2, 0, 1)),
        jnp.transpose(present, (0, 2, 1)),
        owners.reshape(cells),
        targets.reshape(cells),
    )

    def exchange(array):
        return lax.all_to_all(array, "gy", 0, 0, axis_index_groups=along, tiled=True)

    got = exchange(outgoing)
    heads = got[:, FIRST * 32, : SLOTS + 1].astype(jnp.int32)
    tags = heads[:, :SLOTS]
    any_late = jnp.max(heads[:, SLOTS])
    got_late = lax.cond(any_late > 0, exchange, lambda array: array, outgoing_late)
    blocks = across * owned
    dense = pl.pallas_call(
        lambda *refs: gather_kernel(blocks, *refs),
        out_shape=jax.ShapeDtypeStruct((blocks, 32, 128), jnp.bfloat16),
        in_specs=[VMEM, VMEM, SMEM, SMEM],
        out_specs=VMEM,
        scratch_shapes=[pltpu.VMEM((blocks + 1, 32, 128), jnp.float32)],
        compiler_params=PARAMS,
        name="ring_sums",
    )(got, got_late, tags, any_late.reshape(1))
    pieces = lax.all_to_all(
        dense.reshape(across, owned * 32, 128), "gy", 0, 0, axis_index_groups=aside, tiled=True
    )
    coarse = jnp.sum(pieces.astype(jnp.float32), axis=0).astype(jnp.bfloat16)
    return coarse.reshape(1, owned, 32, 128)


def solution(mesh):
    in_specs = (
        P("gx", "gy", None, None),
        P("gx", "gy", None, None),
        P("gx", "gy", None),
        P("gx", "gy", None),
        P("gx", "gy", None),
        P("gx", "gy"),
    )
    out_specs = P("gx", "gy", None, None)
    return jax.shard_map(shards, mesh=mesh, in_specs=in_specs, out_specs=out_specs, check_vma=False)
```

```python
import jax
import jax.numpy as jnp
from jax import lax
from jax.experimental import pallas as pl
from jax.experimental.pallas import tpu as pltpu
from jax.sharding import PartitionSpec as P

RING = 16
SLOTS = 8
FIRST = 6
VMEM = pl.BlockSpec(memory_space=pltpu.VMEM)
ANY = pl.BlockSpec(memory_space=pl.ANY)
CHUNKS = 8
SMEM = pl.BlockSpec(memory_space=pltpu.SMEM)
PARAMS = pltpu.CompilerParams(vmem_limit_bytes=40 * 1024 * 1024)


def unpacked(lines, wide_ref):
    lines = lines.astype(jnp.float32)
    wide_ref[pl.ds(0, 32, stride=2), :] = lines
    wide_ref[pl.ds(1, 32, stride=2), :] = pltpu.roll(lines, 64, 1)
    return wide_ref[...].astype(jnp.bfloat16)


def in_hbm(array):
    return pltpu.with_memory_space_constraint(array, pltpu.HBM)


def edge_kernel(cx, cy, prolong_hbm, near_x_ref, far_x_ref, near_y_ref, far_y_ref, sems):
    even_x = lax.axis_index("gx") % 2 == 0
    even_y = lax.axis_index("gy") % 2 == 0
    copies = [
        pltpu.make_async_copy(prolong_hbm.at[jnp.where(even_x, cx - 1, 0)], near_x_ref, sems.at[0]),
        pltpu.make_async_copy(prolong_hbm.at[jnp.where(even_x, 0, cx - 1)], far_x_ref, sems.at[1]),
        pltpu.make_async_copy(
            prolong_hbm.at[:, jnp.where(even_y, cy - 1, 0)], near_y_ref, sems.at[2]
        ),
        pltpu.make_async_copy(
            prolong_hbm.at[:, jnp.where(even_y, 0, cy - 1)], far_y_ref, sems.at[3]
        ),
    ]
    for copy in copies:
        copy.start()
    for copy in copies:
        copy.wait()


def left_kernel(
    prolong_hbm, couplings_hbm, left_ref, rows_ref, prolong_ref, couplings_ref, wide_ref, sems
):
    size = prolong_hbm.shape[0] // CHUNKS
    fetch = [pltpu.make_async_copy(prolong_hbm, prolong_ref, sems.at[CHUNKS])]
    for chunk in range(CHUNKS):
        part = pl.ds(chunk * size, size)
        fetch.append(
            pltpu.make_async_copy(couplings_hbm.at[part], couplings_ref.at[part], sems.at[chunk])
        )
    for copy in fetch:
        copy.start()
    fetch[0].wait()
    for cell in range(prolong_hbm.shape[0]):
        if cell % size == 0:
            fetch[1 + cell // size].wait()
        rows = unpacked(prolong_ref[cell], wide_ref.at[cell % 4])
        rows_ref[cell] = rows
        product = lax.dot_general(
            rows[:, :64],
            couplings_ref[cell],
            (((0,), (0,)), ((), ())),
            preferred_element_type=jnp.float32,
        ).astype(jnp.bfloat16)
        for d in range(5):
            left_ref[cell, d] = product[:, d * 64 : d * 64 + 64]


def partial_kernel(
    cx,
    cy,
    left_ref,
    rows_ref,
    near_x_ref,
    far_x_ref,
    near_y_ref,
    far_y_ref,
    entries_ref,
    present_ref,
    owners_ref,
    targets_ref,
    out_ref,
    late_ref,
    sums_ref,
    wide_ref,
    slots_ref,
    count_ref,
):
    count = cx * cy
    sums_ref[...] = jnp.zeros_like(sums_ref)

    def add(block, users):
        stack = [left_ref[x * cy + y, d] for x, y, d in users]
        stack = stack[0] if len(stack) == 1 else jnp.concatenate(stack, axis=0)
        terms = jnp.dot(stack, block, preferred_element_type=jnp.float32)
        for n, (x, y, d) in enumerate(users):
            entry = entries_ref[d, x, y]
            if not isinstance(d, int) or d > 0:
                entry = jnp.where(present_ref[x, d - 1, y] != 0, entry, count)
            sums_ref[entry] = sums_ref[entry] + terms[n * 64 : n * 64 + 64]

    for x in range(cx):
        for y in range(cy):
            users = [(x, y, 0), (x - 1, y, 1), (x + 1, y, 2), (x, y - 1, 3), (x, y + 1, 4)]
            users = [u for u in users if 0 <= u[0] < cx and 0 <= u[1] < cy]
            add(rows_ref[x * cy + y], users)
    for axis, far, block_ref in (
        ("gx", 0, near_x_ref),
        ("gx", 1, far_x_ref),
        ("gy", 0, near_y_ref),
        ("gy", 1, far_y_ref),
    ):
        is_next = lax.axis_index(axis) % 2 == far
        for n in range(cy if axis == "gx" else cx):
            block = unpacked(block_ref[n], wide_ref.at[n % 4])
            if axis == "gx":
                user = (jnp.where(is_next, cx - 1, 0), n, jnp.where(is_next, 1, 2))
            else:
                user = (n, jnp.where(is_next, cy - 1, 0), jnp.where(is_next, 3, 4))
            add(block, [user])

    for ring in range(RING):
        count_ref[ring] = 0
    row_id = lax.broadcasted_iota(jnp.int32, (RING, 128), 0)
    lane_id = lax.broadcasted_iota(jnp.int32, (RING, 128), 1)
    low = lax.broadcasted_iota(jnp.int32, (32, 128), 1) < 64
    tags = jnp.full((RING, 128), 128.0, jnp.float32)
    most = jnp.int32(0)
    for e in range(count):
        owner = owners_ref[e]
        ring = owner % RING
        slot = count_ref[ring]
        count_ref[ring] = slot + 1
        even = sums_ref[e, pl.ds(0, 32, stride=2), :]
        odd = sums_ref[e, pl.ds(1, 32, stride=2), :]
        block = jnp.where(low, even, pltpu.roll(odd, 64, 1)).astype(jnp.bfloat16)
        most = jnp.maximum(most, slot)

        slots_ref[ring, pl.ds(pl.multiple_of(slot * 32, 32), 32), :] = block
        tag = (owner // RING) * 16 + targets_ref[e]
        tags = jnp.where((row_id == ring) & (lane_id == slot), tag.astype(jnp.float32), tags)
    late = (most >= FIRST).astype(jnp.float32)
    tags = jnp.where(lane_id == SLOTS, late, tags)
    out_ref[:, : FIRST * 32, :] = slots_ref[:, : FIRST * 32, :]
    late_ref[...] = slots_ref[:, FIRST * 32 :, :]
    for ring in range(RING):
        row = jnp.broadcast_to(tags[ring : ring + 1, :], (16, 128))
        out_ref[ring, FIRST * 32 : FIRST * 32 + 16, :] = row.astype(jnp.bfloat16)


def ring_kernel(blocks, with_late, got_ref, *rest):
    late_ref, (tags_ref, out_ref, any_ref, sums_ref) = rest[0] if with_late else None, rest[-4:]
    sums_ref[...] = jnp.zeros_like(sums_ref)

    def add(ring, slot, from_ref, place):
        tag = jnp.minimum(tags_ref[ring, slot], blocks)
        piece = from_ref[ring, place * 32 : place * 32 + 32, :].astype(jnp.float32)
        sums_ref[tag] = sums_ref[tag] + piece

    for ring in range(RING):
        for slot in range(FIRST):
            add(ring, slot, got_ref, slot)
        if with_late:
            for slot in range(FIRST, SLOTS):
                add(ring, slot, late_ref, slot - FIRST)

    out_ref[...] = sums_ref[:blocks].astype(jnp.bfloat16)
    any_late = tags_ref[0, SLOTS]
    for ring in range(1, RING):
        any_late = jnp.maximum(any_late, tags_ref[ring, SLOTS])
    any_ref[0] = any_late


def shards(couplings, prolong, present, entries, owners, targets):
    cx, cy = prolong.shape[0], prolong.shape[1]
    cells = cx * cy
    across = lax.axis_size("gy") // RING
    along = [[x * RING + z for z in range(RING)] for x in range(across)]
    aside = [[x * RING + z for x in range(across)] for z in range(RING)]
    owned = 16

    edges = pl.pallas_call(
        lambda *refs: edge_kernel(cx, cy, *refs),
        out_shape=(jax.ShapeDtypeStruct((cy, 32, 128), jnp.bfloat16),) * 2
        + (jax.ShapeDtypeStruct((cx, 32, 128), jnp.bfloat16),) * 2,
        in_specs=[ANY],
        out_specs=(ANY,) * 4,
        scratch_shapes=[pltpu.SemaphoreType.DMA((4,))],
        name="edge_blocks",
    )(in_hbm(prolong))

    def swapped(near, far, axis):
        size = lax.axis_size(axis)
        pairs = [(i, i + 1) for i in range(1, size - 1, 2)]
        pairs = pairs + [(j, i) for i, j in pairs]
        return (
            lax.ppermute(near, axis, [(i, i ^ 1) for i in range(size)]),
            lax.ppermute(far, axis, pairs),
        )

    near_x, far_x = swapped(edges[0], edges[1], "gx")
    near_y, far_y = swapped(edges[2], edges[3], "gy")

    left, rows = pl.pallas_call(
        left_kernel,
        out_shape=(
            jax.ShapeDtypeStruct((cells, 5, 64, 64), jnp.bfloat16),
            jax.ShapeDtypeStruct((cells, 64, 128), jnp.bfloat16),
        ),
        in_specs=[ANY, ANY],
        out_specs=(VMEM, VMEM),
        scratch_shapes=[
            pltpu.VMEM((cells, 32, 128), jnp.bfloat16),
            pltpu.VMEM((cells, 64, 320), jnp.bfloat16),
            pltpu.VMEM((4, 64, 128), jnp.float32),
            pltpu.SemaphoreType.DMA((CHUNKS + 1,)),
        ],
        compiler_params=PARAMS,
        cost_estimate=pl.CostEstimate(
            flops=cells * 5 * 2 * 64**3 * 8, bytes_accessed=cells * 90000, transcendentals=0
        ),
        name="left_factor",
    )(in_hbm(prolong.reshape(cells, 32, 128)), in_hbm(couplings.reshape(cells, 64, 320)))

    outgoing, outgoing_late = pl.pallas_call(
        lambda *refs: partial_kernel(cx, cy, *refs),
        out_shape=(
            jax.ShapeDtypeStruct((RING, FIRST * 32 + 16, 128), jnp.bfloat16),
            jax.ShapeDtypeStruct((RING, (SLOTS - FIRST) * 32, 128), jnp.bfloat16),
        ),
        in_specs=[VMEM] * 6 + [SMEM] * 4,
        out_specs=(VMEM, VMEM),
        scratch_shapes=[
            pltpu.VMEM((cells + 1, 64, 128), jnp.float32),
            pltpu.VMEM((4, 64, 128), jnp.float32),
            pltpu.VMEM((RING, SLOTS * 32, 128), jnp.bfloat16),
            pltpu.SMEM((RING,), jnp.int32),
        ],
        compiler_params=PARAMS,
        name="partial_blocks",
    )(
        left,
        rows,
        near_x,
        far_x,
        near_y,
        far_y,
        jnp.transpose(entries, (2, 0, 1)),
        jnp.transpose(present, (0, 2, 1)),
        owners.reshape(cells),
        targets.reshape(cells),
    )

    def exchange(array):
        return lax.all_to_all(array, "gy", 0, 0, axis_index_groups=along, tiled=True)

    got = exchange(outgoing)
    tags = got[:, FIRST * 32, : SLOTS + 1].astype(jnp.int32)
    blocks = across * owned

    def ring_sums(*arrays):
        return pl.pallas_call(
            lambda *refs: ring_kernel(blocks, len(arrays) == 2, *refs),
            out_shape=(
                jax.ShapeDtypeStruct((blocks, 32, 128), jnp.bfloat16),
                jax.ShapeDtypeStruct((1,), jnp.int32),
            ),
            in_specs=[VMEM] * len(arrays) + [SMEM],
            out_specs=(VMEM, SMEM),
            scratch_shapes=[pltpu.VMEM((blocks + 1, 32, 128), jnp.float32)],
            compiler_params=PARAMS,
            name="ring_sums" if len(arrays) == 1 else "ring_sums_late",
        )(*arrays, tags)

    dense, any_late = ring_sums(got)
    dense = lax.cond(
        any_late[0] > 0,
        lambda: ring_sums(got, exchange(outgoing_late))[0],
        lambda: dense,
    )
    pieces = lax.all_to_all(
        dense.reshape(across, owned * 32, 128), "gy", 0, 0, axis_index_groups=aside, tiled=True
    )
    coarse = jnp.sum(pieces.astype(jnp.float32), axis=0).astype(jnp.bfloat16)
    return coarse.reshape(1, owned, 32, 128)


def solution(mesh):
    in_specs = (
        P("gx", "gy", None, None),
        P("gx", "gy", None, None),
        P("gx", "gy", None),
        P("gx", "gy", None),
        P("gx", "gy", None),
        P("gx", "gy"),
    )
    out_specs = P("gx", "gy", None, None)
    return jax.shard_map(shards, mesh=mesh, in_specs=in_specs, out_specs=out_specs, check_vma=False)
```

```python
import jax
import jax.numpy as jnp
from jax import lax
from jax.experimental import pallas as pl
from jax.experimental.pallas import tpu as pltpu
from jax.sharding import PartitionSpec as P

RING = 16
SLOTS = 8
FIRST = 6
VMEM = pl.BlockSpec(memory_space=pltpu.VMEM)
ANY = pl.BlockSpec(memory_space=pl.ANY)
CHUNKS = 8
SMEM = pl.BlockSpec(memory_space=pltpu.SMEM)
PARAMS = pltpu.CompilerParams(vmem_limit_bytes=40 * 1024 * 1024)


def unpacked(lines, wide_ref):
    lines = lines.astype(jnp.float32)
    wide_ref[pl.ds(0, 32, stride=2), :] = lines
    wide_ref[pl.ds(1, 32, stride=2), :] = pltpu.roll(lines, 64, 1)
    return wide_ref[...].astype(jnp.bfloat16)


def in_hbm(array):
    return pltpu.with_memory_space_constraint(array, pltpu.HBM)


def left_kernel(
    prolong_hbm, couplings_hbm, left_ref, rows_ref, prolong_ref, couplings_ref, wide_ref, sems
):
    size = prolong_hbm.shape[0] // CHUNKS
    fetch = [pltpu.make_async_copy(prolong_hbm, prolong_ref, sems.at[CHUNKS])]
    for chunk in range(CHUNKS):
        part = pl.ds(chunk * size, size)
        fetch.append(
            pltpu.make_async_copy(couplings_hbm.at[part], couplings_ref.at[part], sems.at[chunk])
        )
    for copy in fetch:
        copy.start()
    fetch[0].wait()
    for cell in range(prolong_hbm.shape[0]):
        if cell % size == 0:
            fetch[1 + cell // size].wait()
        rows = unpacked(prolong_ref[cell], wide_ref.at[cell % 4])
        rows_ref[cell] = rows
        product = lax.dot_general(
            rows[:, :64],
            couplings_ref[cell],
            (((0,), (0,)), ((), ())),
            preferred_element_type=jnp.float32,
        ).astype(jnp.bfloat16)
        for d in range(5):
            left_ref[cell, d] = product[:, d * 64 : d * 64 + 64]


def partial_kernel(
    cx,
    cy,
    left_ref,
    rows_ref,
    near_x_ref,
    far_x_ref,
    near_y_ref,
    far_y_ref,
    entries_ref,
    present_ref,
    owners_ref,
    targets_ref,
    out_ref,
    late_ref,
    sums_ref,
    wide_ref,
    slots_ref,
    count_ref,
):
    count = cx * cy
    sums_ref[...] = jnp.zeros_like(sums_ref)

    def add(block, users):
        stack = [left_ref[x * cy + y, d] for x, y, d in users]
        stack = stack[0] if len(stack) == 1 else jnp.concatenate(stack, axis=0)
        terms = jnp.dot(stack, block, preferred_element_type=jnp.float32)
        for n, (x, y, d) in enumerate(users):
            entry = entries_ref[d, x, y]
            if not isinstance(d, int) or d > 0:
                entry = jnp.where(present_ref[x, d - 1, y] != 0, entry, count)
            sums_ref[entry] = sums_ref[entry] + terms[n * 64 : n * 64 + 64]

    for x in range(cx):
        for y in range(cy):
            users = [(x, y, 0), (x - 1, y, 1), (x + 1, y, 2), (x, y - 1, 3), (x, y + 1, 4)]
            users = [u for u in users if 0 <= u[0] < cx and 0 <= u[1] < cy]
            add(rows_ref[x * cy + y], users)
    for axis, far, block_ref in (
        ("gx", 0, near_x_ref),
        ("gx", 1, far_x_ref),
        ("gy", 0, near_y_ref),
        ("gy", 1, far_y_ref),
    ):
        is_next = lax.axis_index(axis) % 2 == far
        for n in range(cy if axis == "gx" else cx):
            block = unpacked(block_ref[n], wide_ref.at[n % 4])
            if axis == "gx":
                user = (jnp.where(is_next, cx - 1, 0), n, jnp.where(is_next, 1, 2))
            else:
                user = (n, jnp.where(is_next, cy - 1, 0), jnp.where(is_next, 3, 4))
            add(block, [user])

    for ring in range(RING):
        count_ref[ring] = 0
    row_id = lax.broadcasted_iota(jnp.int32, (RING, 128), 0)
    lane_id = lax.broadcasted_iota(jnp.int32, (RING, 128), 1)
    low = lax.broadcasted_iota(jnp.int32, (32, 128), 1) < 64
    tags = jnp.full((RING, 128), 128.0, jnp.float32)
    most = jnp.int32(0)
    for e in range(count):
        owner = owners_ref[e]
        ring = owner % RING
        slot = count_ref[ring]
        count_ref[ring] = slot + 1
        even = sums_ref[e, pl.ds(0, 32, stride=2), :]
        odd = sums_ref[e, pl.ds(1, 32, stride=2), :]
        block = jnp.where(low, even, pltpu.roll(odd, 64, 1)).astype(jnp.bfloat16)
        most = jnp.maximum(most, slot)

        slots_ref[ring, pl.ds(pl.multiple_of(slot * 32, 32), 32), :] = block
        tag = (owner // RING) * 16 + targets_ref[e]
        tags = jnp.where((row_id == ring) & (lane_id == slot), tag.astype(jnp.float32), tags)
    late = (most >= FIRST).astype(jnp.float32)
    tags = jnp.where(lane_id == SLOTS, late, tags)
    out_ref[:, : FIRST * 32, :] = slots_ref[:, : FIRST * 32, :]
    late_ref[...] = slots_ref[:, FIRST * 32 :, :]
    for ring in range(RING):
        row = jnp.broadcast_to(tags[ring : ring + 1, :], (16, 128))
        out_ref[ring, FIRST * 32 : FIRST * 32 + 16, :] = row.astype(jnp.bfloat16)


def ring_kernel(blocks, with_late, got_ref, *rest):
    late_ref, (tags_ref, out_ref, any_ref, sums_ref) = rest[0] if with_late else None, rest[-4:]
    sums_ref[...] = jnp.zeros_like(sums_ref)

    def add(ring, slot, from_ref, place):
        tag = jnp.minimum(tags_ref[ring, slot], blocks)
        piece = from_ref[ring, place * 32 : place * 32 + 32, :].astype(jnp.float32)
        sums_ref[tag] = sums_ref[tag] + piece

    for ring in range(RING):
        for slot in range(FIRST):
            add(ring, slot, got_ref, slot)
        if with_late:
            for slot in range(FIRST, SLOTS):
                add(ring, slot, late_ref, slot - FIRST)

    out_ref[...] = sums_ref[:blocks].astype(jnp.bfloat16)
    any_late = tags_ref[0, SLOTS]
    for ring in range(1, RING):
        any_late = jnp.maximum(any_late, tags_ref[ring, SLOTS])
    any_ref[0] = any_late


def shards(couplings, prolong, present, entries, owners, targets):
    cx, cy = prolong.shape[0], prolong.shape[1]
    cells = cx * cy
    across = lax.axis_size("gy") // RING
    along = [[x * RING + z for z in range(RING)] for x in range(across)]
    aside = [[x * RING + z for x in range(across)] for z in range(RING)]
    owned = 16

    def swapped(head, tail, axis):
        size = lax.axis_size(axis)
        even = lax.axis_index(axis) % 2 == 0
        near = [(i, i ^ 1) for i in range(size)]
        far = [(i, i + 1) for i in range(1, size - 1, 2)]
        far = far + [(j, i) for i, j in far]
        return (
            lax.ppermute(jnp.where(even, tail, head), axis, near),
            lax.ppermute(jnp.where(even, head, tail), axis, far),
        )

    near_x, far_x = swapped(prolong[0], prolong[cx - 1], "gx")
    near_y, far_y = swapped(prolong[:, 0], prolong[:, cy - 1], "gy")

    left, rows = pl.pallas_call(
        left_kernel,
        out_shape=(
            jax.ShapeDtypeStruct((cells, 5, 64, 64), jnp.bfloat16),
            jax.ShapeDtypeStruct((cells, 64, 128), jnp.bfloat16),
        ),
        in_specs=[ANY, ANY],
        out_specs=(VMEM, VMEM),
        scratch_shapes=[
            pltpu.VMEM((cells, 32, 128), jnp.bfloat16),
            pltpu.VMEM((cells, 64, 320), jnp.bfloat16),
            pltpu.VMEM((4, 64, 128), jnp.float32),
            pltpu.SemaphoreType.DMA((CHUNKS + 1,)),
        ],
        compiler_params=PARAMS,
        cost_estimate=pl.CostEstimate(
            flops=cells * 5 * 2 * 64**3 * 8, bytes_accessed=cells * 90000, transcendentals=0
        ),
        name="left_factor",
    )(in_hbm(prolong.reshape(cells, 32, 128)), in_hbm(couplings.reshape(cells, 64, 320)))

    outgoing, outgoing_late = pl.pallas_call(
        lambda *refs: partial_kernel(cx, cy, *refs),
        out_shape=(
            jax.ShapeDtypeStruct((RING, FIRST * 32 + 16, 128), jnp.bfloat16),
            jax.ShapeDtypeStruct((RING, (SLOTS - FIRST) * 32, 128), jnp.bfloat16),
        ),
        in_specs=[VMEM] * 6 + [SMEM] * 4,
        out_specs=(VMEM, VMEM),
        scratch_shapes=[
            pltpu.VMEM((cells + 1, 64, 128), jnp.float32),
            pltpu.VMEM((4, 64, 128), jnp.float32),
            pltpu.VMEM((RING, SLOTS * 32, 128), jnp.bfloat16),
            pltpu.SMEM((RING,), jnp.int32),
        ],
        compiler_params=PARAMS,
        name="partial_blocks",
    )(
        left,
        rows,
        near_x,
        far_x,
        near_y,
        far_y,
        jnp.transpose(entries, (2, 0, 1)),
        jnp.transpose(present, (0, 2, 1)),
        owners.reshape(cells),
        targets.reshape(cells),
    )

    def exchange(array):
        return lax.all_to_all(array, "gy", 0, 0, axis_index_groups=along, tiled=True)

    got = exchange(outgoing)
    tags = got[:, FIRST * 32, : SLOTS + 1].astype(jnp.int32)
    blocks = across * owned

    def ring_sums(*arrays):
        return pl.pallas_call(
            lambda *refs: ring_kernel(blocks, len(arrays) == 2, *refs),
            out_shape=(
                jax.ShapeDtypeStruct((blocks, 32, 128), jnp.bfloat16),
                jax.ShapeDtypeStruct((1,), jnp.int32),
            ),
            in_specs=[VMEM] * len(arrays) + [SMEM],
            out_specs=(VMEM, SMEM),
            scratch_shapes=[pltpu.VMEM((blocks + 1, 32, 128), jnp.float32)],
            compiler_params=PARAMS,
            name="ring_sums" if len(arrays) == 1 else "ring_sums_late",
        )(*arrays, tags)

    dense, any_late = ring_sums(got)
    dense = lax.cond(
        any_late[0] > 0,
        lambda: ring_sums(got, exchange(outgoing_late))[0],
        lambda: dense,
    )
    pieces = lax.all_to_all(
        dense.reshape(across, owned * 32, 128), "gy", 0, 0, axis_index_groups=aside, tiled=True
    )
    coarse = jnp.sum(pieces.astype(jnp.float32), axis=0).astype(jnp.bfloat16)
    return coarse.reshape(1, owned, 32, 128)


def solution(mesh):
    in_specs = (
        P("gx", "gy", None, None),
        P("gx", "gy", None, None),
        P("gx", "gy", None),
        P("gx", "gy", None),
        P("gx", "gy", None),
        P("gx", "gy"),
    )
    out_specs = P("gx", "gy", None, None)
    return jax.shard_map(shards, mesh=mesh, in_specs=in_specs, out_specs=out_specs, check_vma=False)
```

```python
import jax
import jax.numpy as jnp
from jax import lax
from jax.experimental import pallas as pl
from jax.experimental.pallas import tpu as pltpu
from jax.sharding import PartitionSpec as P

RING = 16
SLOTS = 8
FIRST = 4
VMEM = pl.BlockSpec(memory_space=pltpu.VMEM)
ANY = pl.BlockSpec(memory_space=pl.ANY)
CHUNKS = 8
SMEM = pl.BlockSpec(memory_space=pltpu.SMEM)
PARAMS = pltpu.CompilerParams(vmem_limit_bytes=40 * 1024 * 1024)


def unpacked(lines, wide_ref):
    lines = lines.astype(jnp.float32)
    wide_ref[pl.ds(0, 32, stride=2), :] = lines
    wide_ref[pl.ds(1, 32, stride=2), :] = pltpu.roll(lines, 64, 1)
    return wide_ref[...].astype(jnp.bfloat16)


def in_hbm(array):
    return pltpu.with_memory_space_constraint(array, pltpu.HBM)


def left_kernel(
    prolong_hbm, couplings_hbm, left_ref, rows_ref, prolong_ref, couplings_ref, wide_ref, sems
):
    size = prolong_hbm.shape[0] // CHUNKS
    fetch = [pltpu.make_async_copy(prolong_hbm, prolong_ref, sems.at[CHUNKS])]
    for chunk in range(CHUNKS):
        part = pl.ds(chunk * size, size)
        fetch.append(
            pltpu.make_async_copy(couplings_hbm.at[part], couplings_ref.at[part], sems.at[chunk])
        )
    for copy in fetch:
        copy.start()
    fetch[0].wait()
    for cell in range(prolong_hbm.shape[0]):
        if cell % size == 0:
            fetch[1 + cell // size].wait()
        rows = unpacked(prolong_ref[cell], wide_ref.at[cell % 4])
        rows_ref[cell] = rows
        product = lax.dot_general(
            rows[:, :64],
            couplings_ref[cell],
            (((0,), (0,)), ((), ())),
            preferred_element_type=jnp.float32,
        ).astype(jnp.bfloat16)
        for d in range(5):
            left_ref[cell, d] = product[:, d * 64 : d * 64 + 64]


def partial_kernel(
    cx,
    cy,
    left_ref,
    rows_ref,
    near_x_ref,
    far_x_ref,
    near_y_ref,
    far_y_ref,
    entries_ref,
    present_ref,
    owners_ref,
    targets_ref,
    out_ref,
    late_ref,
    sums_ref,
    wide_ref,
    slots_ref,
    count_ref,
):
    count = cx * cy
    sums_ref[...] = jnp.zeros_like(sums_ref)

    def add(block, users):
        stack = [left_ref[x * cy + y, d] for x, y, d in users]
        stack = stack[0] if len(stack) == 1 else jnp.concatenate(stack, axis=0)
        terms = jnp.dot(stack, block, preferred_element_type=jnp.float32)
        for n, (x, y, d) in enumerate(users):
            entry = entries_ref[d, x, y]
            if not isinstance(d, int) or d > 0:
                entry = jnp.where(present_ref[x, d - 1, y] != 0, entry, count)
            sums_ref[entry] = sums_ref[entry] + terms[n * 64 : n * 64 + 64]

    for x in range(cx):
        for y in range(cy):
            users = [(x, y, 0), (x - 1, y, 1), (x + 1, y, 2), (x, y - 1, 3), (x, y + 1, 4)]
            users = [u for u in users if 0 <= u[0] < cx and 0 <= u[1] < cy]
            add(rows_ref[x * cy + y], users)
    for axis, far, block_ref in (
        ("gx", 0, near_x_ref),
        ("gx", 1, far_x_ref),
        ("gy", 0, near_y_ref),
        ("gy", 1, far_y_ref),
    ):
        is_next = lax.axis_index(axis) % 2 == far
        for n in range(cy if axis == "gx" else cx):
            block = unpacked(block_ref[n], wide_ref.at[n % 4])
            if axis == "gx":
                user = (jnp.where(is_next, cx - 1, 0), n, jnp.where(is_next, 1, 2))
            else:
                user = (n, jnp.where(is_next, cy - 1, 0), jnp.where(is_next, 3, 4))
            add(block, [user])

    for ring in range(RING):
        count_ref[ring] = 0
    row_id = lax.broadcasted_iota(jnp.int32, (RING, 128), 0)
    lane_id = lax.broadcasted_iota(jnp.int32, (RING, 128), 1)
    low = lax.broadcasted_iota(jnp.int32, (32, 128), 1) < 64
    tags = jnp.full((RING, 128), 128.0, jnp.float32)
    most = jnp.int32(0)
    for e in range(count):
        owner = owners_ref[e]
        ring = owner % RING
        slot = count_ref[ring]
        count_ref[ring] = slot + 1
        even = sums_ref[e, pl.ds(0, 32, stride=2), :]
        odd = sums_ref[e, pl.ds(1, 32, stride=2), :]
        block = jnp.where(low, even, pltpu.roll(odd, 64, 1)).astype(jnp.bfloat16)
        most = jnp.maximum(most, slot)

        slots_ref[ring, pl.ds(pl.multiple_of(slot * 32, 32), 32), :] = block
        tag = (owner // RING) * 16 + targets_ref[e]
        tags = jnp.where((row_id == ring) & (lane_id == slot), tag.astype(jnp.float32), tags)
    late = (most >= FIRST).astype(jnp.float32)
    tags = jnp.where(lane_id == SLOTS, late, tags)
    out_ref[:, : FIRST * 32, :] = slots_ref[:, : FIRST * 32, :]
    late_ref[...] = slots_ref[:, FIRST * 32 :, :]
    for ring in range(RING):
        row = jnp.broadcast_to(tags[ring : ring + 1, :], (16, 128))
        out_ref[ring, FIRST * 32 : FIRST * 32 + 16, :] = row.astype(jnp.bfloat16)


def ring_kernel(blocks, with_late, got_ref, *rest):
    late_ref, (tags_ref, out_ref, any_ref, sums_ref) = rest[0] if with_late else None, rest[-4:]
    sums_ref[...] = jnp.zeros_like(sums_ref)

    def add(ring, slot, from_ref, place):
        tag = jnp.minimum(tags_ref[ring, slot], blocks)
        piece = from_ref[ring, place * 32 : place * 32 + 32, :].astype(jnp.float32)
        sums_ref[tag] = sums_ref[tag] + piece

    for ring in range(RING):
        for slot in range(FIRST):
            add(ring, slot, got_ref, slot)
        if with_late:
            for slot in range(FIRST, SLOTS):
                add(ring, slot, late_ref, slot - FIRST)

    out_ref[...] = sums_ref[:blocks].astype(jnp.bfloat16)
    any_late = tags_ref[0, SLOTS]
    for ring in range(1, RING):
        any_late = jnp.maximum(any_late, tags_ref[ring, SLOTS])
    any_ref[0] = any_late


def shards(couplings, prolong, present, entries, owners, targets):
    cx, cy = prolong.shape[0], prolong.shape[1]
    cells = cx * cy
    across = lax.axis_size("gy") // RING
    along = [[x * RING + z for z in range(RING)] for x in range(across)]
    aside = [[x * RING + z for x in range(across)] for z in range(RING)]
    owned = 16

    def swapped(head, tail, axis):
        size = lax.axis_size(axis)
        even = lax.axis_index(axis) % 2 == 0
        near = [(i, i ^ 1) for i in range(size)]
        far = [(i, i + 1) for i in range(1, size - 1, 2)]
        far = far + [(j, i) for i, j in far]
        return (
            lax.ppermute(jnp.where(even, tail, head), axis, near),
            lax.ppermute(jnp.where(even, head, tail), axis, far),
        )

    near_x, far_x = swapped(prolong[0], prolong[cx - 1], "gx")
    near_y, far_y = swapped(prolong[:, 0], prolong[:, cy - 1], "gy")

    left, rows = pl.pallas_call(
        left_kernel,
        out_shape=(
            jax.ShapeDtypeStruct((cells, 5, 64, 64), jnp.bfloat16),
            jax.ShapeDtypeStruct((cells, 64, 128), jnp.bfloat16),
        ),
        in_specs=[ANY, ANY],
        out_specs=(VMEM, VMEM),
        scratch_shapes=[
            pltpu.VMEM((cells, 32, 128), jnp.bfloat16),
            pltpu.VMEM((cells, 64, 320), jnp.bfloat16),
            pltpu.VMEM((4, 64, 128), jnp.float32),
            pltpu.SemaphoreType.DMA((CHUNKS + 1,)),
        ],
        compiler_params=PARAMS,
        cost_estimate=pl.CostEstimate(
            flops=cells * 5 * 2 * 64**3 * 8, bytes_accessed=cells * 90000, transcendentals=0
        ),
        name="left_factor",
    )(in_hbm(prolong.reshape(cells, 32, 128)), in_hbm(couplings.reshape(cells, 64, 320)))

    outgoing, outgoing_late = pl.pallas_call(
        lambda *refs: partial_kernel(cx, cy, *refs),
        out_shape=(
            jax.ShapeDtypeStruct((RING, FIRST * 32 + 16, 128), jnp.bfloat16),
            jax.ShapeDtypeStruct((RING, (SLOTS - FIRST) * 32, 128), jnp.bfloat16),
        ),
        in_specs=[VMEM] * 6 + [SMEM] * 4,
        out_specs=(VMEM, VMEM),
        scratch_shapes=[
            pltpu.VMEM((cells + 1, 64, 128), jnp.float32),
            pltpu.VMEM((4, 64, 128), jnp.float32),
            pltpu.VMEM((RING, SLOTS * 32, 128), jnp.bfloat16),
            pltpu.SMEM((RING,), jnp.int32),
        ],
        compiler_params=PARAMS,
        name="partial_blocks",
    )(
        left,
        rows,
        near_x,
        far_x,
        near_y,
        far_y,
        jnp.transpose(entries, (2, 0, 1)),
        jnp.transpose(present, (0, 2, 1)),
        owners.reshape(cells),
        targets.reshape(cells),
    )

    def exchange(array):
        return lax.all_to_all(array, "gy", 0, 0, axis_index_groups=along, tiled=True)

    got = exchange(outgoing)
    tags = got[:, FIRST * 32, : SLOTS + 1].astype(jnp.int32)
    blocks = across * owned

    def ring_sums(*arrays):
        return pl.pallas_call(
            lambda *refs: ring_kernel(blocks, len(arrays) == 2, *refs),
            out_shape=(
                jax.ShapeDtypeStruct((blocks, 32, 128), jnp.bfloat16),
                jax.ShapeDtypeStruct((1,), jnp.int32),
            ),
            in_specs=[VMEM] * len(arrays) + [SMEM],
            out_specs=(VMEM, SMEM),
            scratch_shapes=[pltpu.VMEM((blocks + 1, 32, 128), jnp.float32)],
            compiler_params=PARAMS,
            name="ring_sums" if len(arrays) == 1 else "ring_sums_late",
        )(*arrays, tags)

    dense, any_late = ring_sums(got)
    dense = lax.cond(
        any_late[0] > 0,
        lambda: ring_sums(got, exchange(outgoing_late))[0],
        lambda: dense,
    )
    pieces = lax.all_to_all(
        dense.reshape(across, owned * 32, 128), "gy", 0, 0, axis_index_groups=aside, tiled=True
    )
    coarse = jnp.sum(pieces.astype(jnp.float32), axis=0).astype(jnp.bfloat16)
    return coarse.reshape(1, owned, 32, 128)


def solution(mesh):
    in_specs = (
        P("gx", "gy", None, None),
        P("gx", "gy", None, None),
        P("gx", "gy", None),
        P("gx", "gy", None),
        P("gx", "gy", None),
        P("gx", "gy"),
    )
    out_specs = P("gx", "gy", None, None)
    return jax.shard_map(shards, mesh=mesh, in_specs=in_specs, out_specs=out_specs, check_vma=False)
```

```python
import jax
import jax.numpy as jnp
from jax import lax
from jax.experimental import pallas as pl
from jax.experimental.pallas import tpu as pltpu
from jax.sharding import PartitionSpec as P

RING = 16
SLOTS = 8
FIRST = 6
VMEM = pl.BlockSpec(memory_space=pltpu.VMEM)
ANY = pl.BlockSpec(memory_space=pl.ANY)
CHUNKS = 8
SMEM = pl.BlockSpec(memory_space=pltpu.SMEM)
PARAMS = pltpu.CompilerParams(vmem_limit_bytes=40 * 1024 * 1024)


def unpacked(lines, wide_ref):
    lines = lines.astype(jnp.float32)
    wide_ref[pl.ds(0, 32, stride=2), :] = lines
    wide_ref[pl.ds(1, 32, stride=2), :] = pltpu.roll(lines, 64, 1)
    return wide_ref[...].astype(jnp.bfloat16)


def in_hbm(array):
    return pltpu.with_memory_space_constraint(array, pltpu.HBM)


def left_kernel(
    prolong_hbm, couplings_hbm, left_ref, rows_ref, prolong_ref, couplings_ref, wide_ref, sems
):
    size = prolong_hbm.shape[0] // CHUNKS
    fetch = [pltpu.make_async_copy(prolong_hbm, prolong_ref, sems.at[CHUNKS])]
    for chunk in range(CHUNKS):
        part = pl.ds(chunk * size, size)
        fetch.append(
            pltpu.make_async_copy(couplings_hbm.at[part], couplings_ref.at[part], sems.at[chunk])
        )
    for copy in fetch:
        copy.start()
    fetch[0].wait()
    for cell in range(prolong_hbm.shape[0]):
        if cell % size == 0:
            fetch[1 + cell // size].wait()
        rows = unpacked(prolong_ref[cell], wide_ref.at[cell % 4])
        rows_ref[cell] = rows
        product = lax.dot_general(
            rows[:, :64],
            couplings_ref[cell],
            (((0,), (0,)), ((), ())),
            preferred_element_type=jnp.float32,
        ).astype(jnp.bfloat16)
        for d in range(5):
            left_ref[cell, d] = product[:, d * 64 : d * 64 + 64]


def partial_kernel(
    cx,
    cy,
    sizes,
    left_ref,
    rows_ref,
    near_x_ref,
    far_x_ref,
    near_y_ref,
    far_y_ref,
    entries_ref,
    present_ref,
    owners_ref,
    targets_ref,
    out_ref,
    late_ref,
    sums_ref,
    wide_ref,
    slots_ref,
    count_ref,
):
    count = cx * cy
    sums_ref[...] = jnp.zeros_like(sums_ref)

    def add(block, users, outside=False):
        stack = [left_ref[x * cy + y, d] for x, y, d in users]
        stack = stack[0] if len(stack) == 1 else jnp.concatenate(stack, axis=0)
        terms = jnp.dot(stack, block, preferred_element_type=jnp.float32)
        for n, (x, y, d) in enumerate(users):
            entry = entries_ref[d, x, y]
            if not isinstance(d, int) or d > 0:
                entry = jnp.where(present_ref[x, d - 1, y] != 0, entry, count)
            if outside is not False:
                entry = jnp.where(outside, count, entry)
            sums_ref[entry] = sums_ref[entry] + terms[n * 64 : n * 64 + 64]

    for x in range(cx):
        for y in range(cy):
            users = [(x, y, 0), (x - 1, y, 1), (x + 1, y, 2), (x, y - 1, 3), (x, y + 1, 4)]
            users = [u for u in users if 0 <= u[0] < cx and 0 <= u[1] < cy]
            add(rows_ref[x * cy + y], users)
    for axis, far, block_ref in (
        ("gx", 0, near_x_ref),
        ("gx", 1, far_x_ref),
        ("gy", 0, near_y_ref),
        ("gy", 1, far_y_ref),
    ):
        index = lax.axis_index(axis)
        is_next = index % 2 == far
        outside = ((index == 0) | (index == sizes[axis] - 1)) if far else False
        for n in range(cy if axis == "gx" else cx):
            block = unpacked(block_ref[n], wide_ref.at[n % 4])
            if axis == "gx":
                user = (jnp.where(is_next, cx - 1, 0), n, jnp.where(is_next, 1, 2))
            else:
                user = (n, jnp.where(is_next, cy - 1, 0), jnp.where(is_next, 3, 4))
            add(block, [user], outside)

    for ring in range(RING):
        count_ref[ring] = 0
    row_id = lax.broadcasted_iota(jnp.int32, (RING, 128), 0)
    lane_id = lax.broadcasted_iota(jnp.int32, (RING, 128), 1)
    low = lax.broadcasted_iota(jnp.int32, (32, 128), 1) < 64
    tags = jnp.full((RING, 128), 128.0, jnp.float32)
    most = jnp.int32(0)
    for e in range(count):
        owner = owners_ref[e]
        ring = owner % RING
        slot = count_ref[ring]
        count_ref[ring] = slot + 1
        even = sums_ref[e, pl.ds(0, 32, stride=2), :]
        odd = sums_ref[e, pl.ds(1, 32, stride=2), :]
        block = jnp.where(low, even, pltpu.roll(odd, 64, 1)).astype(jnp.bfloat16)
        most = jnp.maximum(most, slot)

        slots_ref[ring, pl.ds(pl.multiple_of(slot * 32, 32), 32), :] = block
        tag = (owner // RING) * 16 + targets_ref[e]
        tags = jnp.where((row_id == ring) & (lane_id == slot), tag.astype(jnp.float32), tags)
    late = (most >= FIRST).astype(jnp.float32)
    tags = jnp.where(lane_id == SLOTS, late, tags)
    out_ref[:, : FIRST * 32, :] = slots_ref[:, : FIRST * 32, :]
    late_ref[...] = slots_ref[:, FIRST * 32 :, :]
    for ring in range(RING):
        row = jnp.broadcast_to(tags[ring : ring + 1, :], (16, 128))
        out_ref[ring, FIRST * 32 : FIRST * 32 + 16, :] = row.astype(jnp.bfloat16)


def ring_kernel(blocks, with_late, got_ref, *rest):
    late_ref, (tags_ref, out_ref, any_ref, sums_ref) = rest[0] if with_late else None, rest[-4:]
    sums_ref[...] = jnp.zeros_like(sums_ref)

    def add(ring, slot, from_ref, place):
        tag = jnp.minimum(tags_ref[ring, slot], blocks)
        piece = from_ref[ring, place * 32 : place * 32 + 32, :].astype(jnp.float32)
        sums_ref[tag] = sums_ref[tag] + piece

    for ring in range(RING):
        for slot in range(FIRST):
            add(ring, slot, got_ref, slot)
        if with_late:
            for slot in range(FIRST, SLOTS):
                add(ring, slot, late_ref, slot - FIRST)

    out_ref[...] = sums_ref[:blocks].astype(jnp.bfloat16)
    any_late = tags_ref[0, SLOTS]
    for ring in range(1, RING):
        any_late = jnp.maximum(any_late, tags_ref[ring, SLOTS])
    any_ref[0] = any_late


def shards(couplings, prolong, present, entries, owners, targets):
    cx, cy = prolong.shape[0], prolong.shape[1]
    cells = cx * cy
    sizes = {axis: lax.axis_size(axis) for axis in ("gx", "gy")}
    across = lax.axis_size("gy") // RING
    along = [[x * RING + z for z in range(RING)] for x in range(across)]
    aside = [[x * RING + z for x in range(across)] for z in range(RING)]
    owned = 16

    def swapped(head, tail, axis):
        size = lax.axis_size(axis)
        even = lax.axis_index(axis) % 2 == 0
        near = [(i, i ^ 1) for i in range(size)]
        far = [(i, (i + 1 if i % 2 else i - 1) % size) for i in range(size)]
        return (
            lax.ppermute(jnp.where(even, tail, head), axis, near),
            lax.ppermute(jnp.where(even, head, tail), axis, far),
        )

    near_x, far_x = swapped(prolong[0], prolong[cx - 1], "gx")
    near_y, far_y = swapped(prolong[:, 0], prolong[:, cy - 1], "gy")

    left, rows = pl.pallas_call(
        left_kernel,
        out_shape=(
            jax.ShapeDtypeStruct((cells, 5, 64, 64), jnp.bfloat16),
            jax.ShapeDtypeStruct((cells, 64, 128), jnp.bfloat16),
        ),
        in_specs=[ANY, ANY],
        out_specs=(VMEM, VMEM),
        scratch_shapes=[
            pltpu.VMEM((cells, 32, 128), jnp.bfloat16),
            pltpu.VMEM((cells, 64, 320), jnp.bfloat16),
            pltpu.VMEM((4, 64, 128), jnp.float32),
            pltpu.SemaphoreType.DMA((CHUNKS + 1,)),
        ],
        compiler_params=PARAMS,
        cost_estimate=pl.CostEstimate(
            flops=cells * 5 * 2 * 64**3 * 8, bytes_accessed=cells * 90000, transcendentals=0
        ),
        name="left_factor",
    )(in_hbm(prolong.reshape(cells, 32, 128)), in_hbm(couplings.reshape(cells, 64, 320)))

    outgoing, outgoing_late = pl.pallas_call(
        lambda *refs: partial_kernel(cx, cy, sizes, *refs),
        out_shape=(
            jax.ShapeDtypeStruct((RING, FIRST * 32 + 16, 128), jnp.bfloat16),
            jax.ShapeDtypeStruct((RING, (SLOTS - FIRST) * 32, 128), jnp.bfloat16),
        ),
        in_specs=[VMEM] * 6 + [SMEM] * 4,
        out_specs=(VMEM, VMEM),
        scratch_shapes=[
            pltpu.VMEM((cells + 1, 64, 128), jnp.float32),
            pltpu.VMEM((4, 64, 128), jnp.float32),
            pltpu.VMEM((RING, SLOTS * 32, 128), jnp.bfloat16),
            pltpu.SMEM((RING,), jnp.int32),
        ],
        compiler_params=PARAMS,
        name="partial_blocks",
    )(
        left,
        rows,
        near_x,
        far_x,
        near_y,
        far_y,
        jnp.transpose(entries, (2, 0, 1)),
        jnp.transpose(present, (0, 2, 1)),
        owners.reshape(cells),
        targets.reshape(cells),
    )

    def exchange(array):
        return lax.all_to_all(array, "gy", 0, 0, axis_index_groups=along, tiled=True)

    got = exchange(outgoing)
    tags = got[:, FIRST * 32, : SLOTS + 1].astype(jnp.int32)
    blocks = across * owned

    def ring_sums(*arrays):
        return pl.pallas_call(
            lambda *refs: ring_kernel(blocks, len(arrays) == 2, *refs),
            out_shape=(
                jax.ShapeDtypeStruct((blocks, 32, 128), jnp.bfloat16),
                jax.ShapeDtypeStruct((1,), jnp.int32),
            ),
            in_specs=[VMEM] * len(arrays) + [SMEM],
            out_specs=(VMEM, SMEM),
            scratch_shapes=[pltpu.VMEM((blocks + 1, 32, 128), jnp.float32)],
            compiler_params=PARAMS,
            name="ring_sums" if len(arrays) == 1 else "ring_sums_late",
        )(*arrays, tags)

    dense, any_late = ring_sums(got)
    dense = lax.cond(
        any_late[0] > 0,
        lambda: ring_sums(got, exchange(outgoing_late))[0],
        lambda: dense,
    )
    pieces = lax.all_to_all(
        dense.reshape(across, owned * 32, 128), "gy", 0, 0, axis_index_groups=aside, tiled=True
    )
    coarse = jnp.sum(pieces.astype(jnp.float32), axis=0).astype(jnp.bfloat16)
    return coarse.reshape(1, owned, 32, 128)


def solution(mesh):
    in_specs = (
        P("gx", "gy", None, None),
        P("gx", "gy", None, None),
        P("gx", "gy", None),
        P("gx", "gy", None),
        P("gx", "gy", None),
        P("gx", "gy"),
    )
    out_specs = P("gx", "gy", None, None)
    return jax.shard_map(shards, mesh=mesh, in_specs=in_specs, out_specs=out_specs, check_vma=False)
```

```python
import jax
import jax.numpy as jnp
from jax import lax
from jax.experimental import pallas as pl
from jax.experimental.pallas import tpu as pltpu
from jax.sharding import PartitionSpec as P

RING = 16
SLOTS = 8
FIRST = 6
VMEM = pl.BlockSpec(memory_space=pltpu.VMEM)
ANY = pl.BlockSpec(memory_space=pl.ANY)
CHUNKS = 8
SMEM = pl.BlockSpec(memory_space=pltpu.SMEM)
PARAMS = pltpu.CompilerParams(vmem_limit_bytes=40 * 1024 * 1024)


def unpacked(lines, wide_ref):
    lines = lines.astype(jnp.float32)
    wide_ref[pl.ds(0, 32, stride=2), :] = lines
    wide_ref[pl.ds(1, 32, stride=2), :] = pltpu.roll(lines, 64, 1)
    return wide_ref[...].astype(jnp.bfloat16)


def in_hbm(array):
    return pltpu.with_memory_space_constraint(array, pltpu.HBM)


def left_kernel(
    prolong_hbm, couplings_hbm, left_ref, rows_ref, prolong_ref, couplings_ref, wide_ref, sems
):
    size = prolong_hbm.shape[0] // CHUNKS
    fetch = [pltpu.make_async_copy(prolong_hbm, prolong_ref, sems.at[CHUNKS])]
    for chunk in range(CHUNKS):
        part = pl.ds(chunk * size, size)
        fetch.append(
            pltpu.make_async_copy(couplings_hbm.at[part], couplings_ref.at[part], sems.at[chunk])
        )
    for copy in fetch:
        copy.start()
    fetch[0].wait()
    for cell in range(prolong_hbm.shape[0]):
        if cell % size == 0:
            fetch[1 + cell // size].wait()
        rows = unpacked(prolong_ref[cell], wide_ref.at[cell])
        rows_ref[cell] = rows
        product = lax.dot_general(
            rows[:, :64],
            couplings_ref[cell],
            (((0,), (0,)), ((), ())),
            preferred_element_type=jnp.float32,
        ).astype(jnp.bfloat16)
        for d in range(5):
            left_ref[cell, d] = product[:, d * 64 : d * 64 + 64]


def partial_kernel(
    cx,
    cy,
    sizes,
    left_ref,
    rows_ref,
    near_x_ref,
    far_x_ref,
    near_y_ref,
    far_y_ref,
    entries_ref,
    present_ref,
    owners_ref,
    targets_ref,
    out_ref,
    late_ref,
    sums_ref,
    wide_ref,
    slots_ref,
    count_ref,
):
    count = cx * cy
    sums_ref[...] = jnp.zeros_like(sums_ref)

    def add(block, users, outside=False):
        stack = [left_ref[x * cy + y, d] for x, y, d in users]
        stack = stack[0] if len(stack) == 1 else jnp.concatenate(stack, axis=0)
        terms = jnp.dot(stack, block, preferred_element_type=jnp.float32)
        for n, (x, y, d) in enumerate(users):
            entry = entries_ref[d, x, y]
            if not isinstance(d, int) or d > 0:
                entry = jnp.where(present_ref[x, d - 1, y] != 0, entry, count)
            if outside is not False:
                entry = jnp.where(outside, count, entry)
            sums_ref[entry] = sums_ref[entry] + terms[n * 64 : n * 64 + 64]

    for x in range(cx):
        for y in range(cy):
            users = [(x, y, 0), (x - 1, y, 1), (x + 1, y, 2), (x, y - 1, 3), (x, y + 1, 4)]
            users = [u for u in users if 0 <= u[0] < cx and 0 <= u[1] < cy]
            add(rows_ref[x * cy + y], users)
    used = 0
    for axis, far, block_ref in (
        ("gx", 0, near_x_ref),
        ("gx", 1, far_x_ref),
        ("gy", 0, near_y_ref),
        ("gy", 1, far_y_ref),
    ):
        index = lax.axis_index(axis)
        is_next = index % 2 == far
        outside = ((index == 0) | (index == sizes[axis] - 1)) if far else False
        for n in range(cy if axis == "gx" else cx):
            block = unpacked(block_ref[n], wide_ref.at[used])
            used += 1
            if axis == "gx":
                user = (jnp.where(is_next, cx - 1, 0), n, jnp.where(is_next, 1, 2))
            else:
                user = (n, jnp.where(is_next, cy - 1, 0), jnp.where(is_next, 3, 4))
            add(block, [user], outside)

    for ring in range(RING):
        count_ref[ring] = 0
    row_id = lax.broadcasted_iota(jnp.int32, (RING, 128), 0)
    lane_id = lax.broadcasted_iota(jnp.int32, (RING, 128), 1)
    low = lax.broadcasted_iota(jnp.int32, (32, 128), 1) < 64
    tags = jnp.full((RING, 128), 128.0, jnp.float32)
    most = jnp.int32(0)
    for e in range(count):
        owner = owners_ref[e]
        ring = owner % RING
        slot = count_ref[ring]
        count_ref[ring] = slot + 1
        even = sums_ref[e, pl.ds(0, 32, stride=2), :]
        odd = sums_ref[e, pl.ds(1, 32, stride=2), :]
        block = jnp.where(low, even, pltpu.roll(odd, 64, 1)).astype(jnp.bfloat16)
        most = jnp.maximum(most, slot)

        slots_ref[ring, pl.ds(pl.multiple_of(slot * 32, 32), 32), :] = block
        tag = (owner // RING) * 16 + targets_ref[e]
        tags = jnp.where((row_id == ring) & (lane_id == slot), tag.astype(jnp.float32), tags)
    late = (most >= FIRST).astype(jnp.float32)
    tags = jnp.where(lane_id == SLOTS, late, tags)
    out_ref[:, : FIRST * 32, :] = slots_ref[:, : FIRST * 32, :]
    late_ref[...] = slots_ref[:, FIRST * 32 :, :]
    for ring in range(RING):
        row = jnp.broadcast_to(tags[ring : ring + 1, :], (16, 128))
        out_ref[ring, FIRST * 32 : FIRST * 32 + 16, :] = row.astype(jnp.bfloat16)


def ring_kernel(blocks, with_late, got_ref, *rest):
    late_ref, (tags_ref, out_ref, any_ref, sums_ref) = rest[0] if with_late else None, rest[-4:]
    sums_ref[...] = jnp.zeros_like(sums_ref)

    def add(ring, slot, from_ref, place):
        tag = jnp.minimum(tags_ref[ring, slot], blocks)
        piece = from_ref[ring, place * 32 : place * 32 + 32, :].astype(jnp.float32)
        sums_ref[tag] = sums_ref[tag] + piece

    for ring in range(RING):
        for slot in range(FIRST):
            add(ring, slot, got_ref, slot)
        if with_late:
            for slot in range(FIRST, SLOTS):
                add(ring, slot, late_ref, slot - FIRST)

    out_ref[...] = sums_ref[:blocks].astype(jnp.bfloat16)
    any_late = tags_ref[0, SLOTS]
    for ring in range(1, RING):
        any_late = jnp.maximum(any_late, tags_ref[ring, SLOTS])
    any_ref[0] = any_late


def shards(couplings, prolong, present, entries, owners, targets):
    cx, cy = prolong.shape[0], prolong.shape[1]
    cells = cx * cy
    sizes = {axis: lax.axis_size(axis) for axis in ("gx", "gy")}
    across = lax.axis_size("gy") // RING
    along = [[x * RING + z for z in range(RING)] for x in range(across)]
    aside = [[x * RING + z for x in range(across)] for z in range(RING)]
    owned = 16

    def swapped(head, tail, axis):
        size = lax.axis_size(axis)
        even = lax.axis_index(axis) % 2 == 0
        near = [(i, i ^ 1) for i in range(size)]
        far = [(i, (i + 1 if i % 2 else i - 1) % size) for i in range(size)]
        return (
            lax.ppermute(jnp.where(even, tail, head), axis, near),
            lax.ppermute(jnp.where(even, head, tail), axis, far),
        )

    near_x, far_x = swapped(prolong[0], prolong[cx - 1], "gx")
    near_y, far_y = swapped(prolong[:, 0], prolong[:, cy - 1], "gy")

    left, rows = pl.pallas_call(
        left_kernel,
        out_shape=(
            jax.ShapeDtypeStruct((cells, 5, 64, 64), jnp.bfloat16),
            jax.ShapeDtypeStruct((cells, 64, 128), jnp.bfloat16),
        ),
        in_specs=[ANY, ANY],
        out_specs=(VMEM, VMEM),
        scratch_shapes=[
            pltpu.VMEM((cells, 32, 128), jnp.bfloat16),
            pltpu.VMEM((cells, 64, 320), jnp.bfloat16),
            pltpu.VMEM((cells, 64, 128), jnp.float32),
            pltpu.SemaphoreType.DMA((CHUNKS + 1,)),
        ],
        compiler_params=PARAMS,
        cost_estimate=pl.CostEstimate(
            flops=cells * 5 * 2 * 64**3 * 8, bytes_accessed=cells * 90000, transcendentals=0
        ),
        name="left_factor",
    )(in_hbm(prolong.reshape(cells, 32, 128)), in_hbm(couplings.reshape(cells, 64, 320)))

    outgoing, outgoing_late = pl.pallas_call(
        lambda *refs: partial_kernel(cx, cy, sizes, *refs),
        out_shape=(
            jax.ShapeDtypeStruct((RING, FIRST * 32 + 16, 128), jnp.bfloat16),
            jax.ShapeDtypeStruct((RING, (SLOTS - FIRST) * 32, 128), jnp.bfloat16),
        ),
        in_specs=[VMEM] * 6 + [SMEM] * 4,
        out_specs=(VMEM, VMEM),
        scratch_shapes=[
            pltpu.VMEM((cells + 1, 64, 128), jnp.float32),
            pltpu.VMEM((2 * (cx + cy), 64, 128), jnp.float32),
            pltpu.VMEM((RING, SLOTS * 32, 128), jnp.bfloat16),
            pltpu.SMEM((RING,), jnp.int32),
        ],
        compiler_params=PARAMS,
        name="partial_blocks",
    )(
        left,
        rows,
        near_x,
        far_x,
        near_y,
        far_y,
        jnp.transpose(entries, (2, 0, 1)),
        jnp.transpose(present, (0, 2, 1)),
        owners.reshape(cells),
        targets.reshape(cells),
    )

    def exchange(array):
        return lax.all_to_all(array, "gy", 0, 0, axis_index_groups=along, tiled=True)

    got = exchange(outgoing)
    tags = got[:, FIRST * 32, : SLOTS + 1].astype(jnp.int32)
    blocks = across * owned

    def ring_sums(*arrays):
        return pl.pallas_call(
            lambda *refs: ring_kernel(blocks, len(arrays) == 2, *refs),
            out_shape=(
                jax.ShapeDtypeStruct((blocks, 32, 128), jnp.bfloat16),
                jax.ShapeDtypeStruct((1,), jnp.int32),
            ),
            in_specs=[VMEM] * len(arrays) + [SMEM],
            out_specs=(VMEM, SMEM),
            scratch_shapes=[pltpu.VMEM((blocks + 1, 32, 128), jnp.float32)],
            compiler_params=PARAMS,
            name="ring_sums" if len(arrays) == 1 else "ring_sums_late",
        )(*arrays, tags)

    dense, any_late = ring_sums(got)
    dense = lax.cond(
        any_late[0] > 0,
        lambda: ring_sums(got, exchange(outgoing_late))[0],
        lambda: dense,
    )
    pieces = lax.all_to_all(
        dense.reshape(across, owned * 32, 128), "gy", 0, 0, axis_index_groups=aside, tiled=True
    )
    coarse = jnp.sum(pieces.astype(jnp.float32), axis=0).astype(jnp.bfloat16)
    return coarse.reshape(1, owned, 32, 128)


def solution(mesh):
    in_specs = (
        P("gx", "gy", None, None),
        P("gx", "gy", None, None),
        P("gx", "gy", None),
        P("gx", "gy", None),
        P("gx", "gy", None),
        P("gx", "gy"),
    )
    out_specs = P("gx", "gy", None, None)
    return jax.shard_map(shards, mesh=mesh, in_specs=in_specs, out_specs=out_specs, check_vma=False)
```
